256 devices in a mesh: dp: 32 (over x, z), expert: 8 (over y, core).
Axes of the slice: x: 4, y: 4, z: 8, core: 2. Of those that a mesh axis runs over, the one named last changes fastest.
Arguments:
- tokens: bfloat16 [32768, 2048], P(('dp', 'expert')), may hold values from -6 to 6
- cotangent: bfloat16 [32768, 2048], P(('dp', 'expert')), may hold values from -6 to 6
- down_vectors: bfloat16 [120, 64, 2048], P('expert'), may hold values from -0.125 to 0.125
- up_vectors: bfloat16 [120, 64, 2048], P('expert'), may hold values from -0.1875 to 0.1875
- block_ids: int32 [256, 16], P(('dp', 'expert')), may hold values from 0 to 119, as said below
Outputs:
- output: bfloat16 [32768, 2048], P(('dp', 'expert'))
- input_grad: bfloat16 [32768, 2048], P(('dp', 'expert'))
- down_grad: float32 [120, 64, 2048], P('expert', None, 'dp')
- up_grad: float32 [120, 64, 2048], P('expert', None, 'dp')
The draws below stay inside these ranges and needn't reach their ends.
Inputs may be any that keep to these rules, and one draw needn't show every extreme that they name: `block_ids`: the 16 ids of one tile are distinct. At most 4 of them lie in one slab (ids s * 15 to (s + 1) * 15 - 1), and every tile has exactly 4 in some slab.
All inputs are finite; a program needn't handle non-finite values.
Results may differ from the reference program's by a relative error of at most 0.02.
Values may be sent and summed in bfloat16 or wider, within the bound.
A program may use at most 192 MiB of HBM per device.

```python
import jax
import jax.numpy as jnp
from jax import lax

D = 2048
BS = 64
SEL = 16
BLK_DEV = 15
TILE = 128
MOST = 4
BLOCKS = 120
TOKENS = 32768
TILES = 256
N_EXPERT = 8


def draw_block_ids(key, part):
    key = jax.random.fold_in(key, 11)
    rank_index = jnp.arange(N_EXPERT, dtype=jnp.int32)
    remaining = SEL - MOST
    other_slabs = N_EXPERT - 1
    counts = jnp.where(rank_index == 0, MOST, remaining // other_slabs + (rank_index - 1 < remaining % other_slabs).astype(jnp.int32)).astype(jnp.int32)
    run_ends = jnp.cumsum(counts).astype(jnp.int32)
    run_starts = run_ends - counts
    position = jnp.arange(SEL, dtype=jnp.int32)
    run_of = jnp.sum((run_ends[None, :] <= position[:, None]).astype(jnp.int32), axis=1)
    offset = position - run_starts[run_of]

    def shuffle_slab(slab_key):
        return jax.random.permutation(slab_key, BLK_DEV)

    def one_tile(tile_key):
        sub_keys = jax.random.split(tile_key, N_EXPERT + 2)
        slab_order = jax.random.permutation(sub_keys[0], N_EXPERT)
        inner_order = jax.vmap(shuffle_slab)(sub_keys[2:])
        chosen = slab_order[run_of] * BLK_DEV + inner_order[run_of, offset]
        return chosen[jax.random.permutation(sub_keys[1], SEL)]
    tile_keys = jax.random.split(key, TILES)
    return jax.vmap(one_tile)(tile_keys).astype(jnp.int32)


def steps_of(stream_key, shape, shards, smallest, top_value):
    factor_of = 1.0
    for dim, shards_of in shards:
        draws = jax.random.uniform(jax.random.fold_in(jax.random.fold_in(stream_key, 6), dim), (shards_of,), jnp.float32, smallest / len(shards), top_value / len(shards))
        factor_of = factor_of * jnp.repeat(jnp.exp(draws), shape[dim] // shards_of).reshape((-1,) + (1,) * (len(shape) - 1 - dim))
    return factor_of


def centred(own_key, dims, spread, most, cuts=(), held_as=jnp.bfloat16):
    values = jax.random.normal(own_key, dims, jnp.float32) * spread
    if len(cuts) > 0:
        values = steps_of(own_key, dims, cuts, -0.22, 0.18) * values
    return jnp.clip(values, min=-most, max=most).astype(held_as)


def setup_inputs(seed: int = 0) -> dict:
    arg_keys = jax.random.split(jax.random.key(seed), 6)
    return {
        "tokens": centred(arg_keys[0], (TOKENS, D), 1.0, 6.0, ((0, 256),)),
        "cotangent": centred(arg_keys[1], (TOKENS, D), 1.0, 6.0, ((0, 256),)),
        "down_vectors": centred(arg_keys[2], (BLOCKS, BS, D), D ** -0.5, 0.125, ((0, 8),)),
        "up_vectors": centred(arg_keys[3], (BLOCKS, BS, D), (SEL * BS) ** -0.5, 0.1875, ((0, 8),)),
        "block_ids": draw_block_ids(jax.random.fold_in(arg_keys[5], 71), 0),
    }


def silu_slope(argument):
    sigmoid_val = jax.nn.sigmoid(argument)
    return sigmoid_val * (1.0 + argument * (1.0 - sigmoid_val))


def reference(tokens, cotangent, down_vectors, up_vectors, block_ids):
    highest = lax.Precision.HIGHEST
    tok_tiles = tokens.reshape(TILES, TILE, D)
    cot_tiles = cotangent.reshape(TILES, TILE, D)
    slab_index = jnp.arange(N_EXPERT, dtype=jnp.int32)

    def one_tile(totals, inputs):
        down_acc, up_acc = totals
        tile_tok, tile_cot, block_row = inputs
        block_row = block_row.astype(jnp.int32)
        down_sel = jnp.take(down_vectors, block_row, axis=0).astype(jnp.float32)
        up_sel = jnp.take(up_vectors, block_row, axis=0).astype(jnp.float32)
        owner_slab = (block_row // BLK_DEV).astype(jnp.int32)
        member = (owner_slab[:, None] == slab_index[None, :]).astype(jnp.float32)
        tok_float = tile_tok.astype(jnp.float32)
        cot_float = tile_cot.astype(jnp.float32)
        scores = jnp.einsum("td,jed->tje", tok_float, down_sel, precision=highest)
        hidden = jax.nn.silu(scores).astype(jnp.bfloat16)
        hid_float = hidden.astype(jnp.float32)
        out_partial = jnp.einsum("tje,js,jed->std", hid_float, member, up_sel, precision=highest)
        out_partial = lax.optimization_barrier(out_partial.astype(jnp.bfloat16))
        out_tile = jnp.sum(out_partial.astype(jnp.float32), axis=0).astype(jnp.bfloat16)
        back_hidden = jnp.einsum("td,jed->tje", cot_float, up_sel, precision=highest)
        back_scores = (back_hidden * silu_slope(scores)).astype(jnp.bfloat16)
        back_float = back_scores.astype(jnp.float32)
        in_partial = jnp.einsum("tje,js,jed->std", back_float, member, down_sel, precision=highest)
        in_partial = lax.optimization_barrier(in_partial.astype(jnp.bfloat16))
        in_tile = jnp.sum(in_partial.astype(jnp.float32), axis=0).astype(jnp.bfloat16)
        down_acc = down_acc.at[block_row].add(jnp.einsum("tje,td->jed", back_float, tok_float, precision=highest))
        up_acc = up_acc.at[block_row].add(jnp.einsum("tje,td->jed", hid_float, cot_float, precision=highest))
        return (down_acc, up_acc), (out_tile, in_tile)

    empty_grads = jnp.zeros((BLOCKS, BS, D), jnp.float32)
    grads, tiles_out = lax.scan(one_tile, (empty_grads, empty_grads), (tok_tiles, cot_tiles, block_ids))
    out_tiles, in_tiles = tiles_out
    return (out_tiles.reshape(TILES * TILE, D), in_tiles.reshape(TILES * TILE, D), grads[0], grads[1])
```

```python
import functools

import jax
import jax.numpy as jnp
from jax import lax
from jax.experimental import pallas as pl
from jax.experimental.pallas import tpu as pltpu
from jax.sharding import PartitionSpec as P

MESH = pl.DeviceIdType.MESH
BF16 = jnp.bfloat16
F32 = jnp.float32
ROWS_PAD = 1024
ZSIZE = 8
TOP, BOTTOM = pl.ds(0, 64), pl.ds(64, 64)
CHUNKS = (
    ("x", 1, (0, 1)),
    ("z", 1, (2, 3)),
    ("x", 1, (4, 5)),
    ("z", 0, (0, 1)),
    ("x", 0, (2, 3)),
    ("z", 0, (4, 5)),
    ("x", 0, (6,)),
    ("x", 1, (6,)),
    ("x", 2, (7,)),
)


def kernel(xs, zs, *refs):
    ids, tok, cot, dn, up, out_o, in_o, dg_o, ug_o = refs[:9]
    dnv, upv, A, T, HB, pres, sibR, R1, R2 = refs[9:18]
    rest = refs[18:]
    grads = [rest[3 * i : 3 * i + 3] for i in range(len(CHUNKS))]
    ssem, rsem, lsem = rest[3 * len(CHUNKS) :]
    width = tok.shape[1]
    slab_rows = dn.shape[0]

    dp, e = lax.axis_index("dp"), lax.axis_index("expert")
    x, z = dp // zs, dp % zs
    y, k = e // 2, e % 2
    yp = (dp, ((y + 1) % 4) * 2 + k)
    ym = (dp, ((y + 3) % 4) * 2 + k)
    sib = (dp, y * 2 + (1 - k))
    near = {
        "x": ((((x + 1) % xs) * zs + z, e), (((x + xs - 1) % xs) * zs + z, e)),
        "z": ((x * zs + (z + 1) % zs, e), (x * zs + (z + zs - 1) % zs, e)),
    }
    spot = {"x": (x, xs), "z": (z, zs)}

    started = []

    def send(src, dst, dev):
        i = len(started)
        c = pltpu.make_async_remote_copy(
            src_ref=src, dst_ref=dst, send_sem=ssem.at[i], recv_sem=rsem.at[i],
            device_id=dev, device_id_type=MESH,
        )
        c.start()
        started.append([c, True])
        return i

    def arrived(i):
        started[i][0].wait_recv()

    def sent(i):
        if started[i][1]:
            started[i][1] = False
            started[i][0].wait_send()

    def local(src, dst, i):
        c = pltpu.make_async_copy(src, dst, lsem.at[i])
        c.start()
        return c

    barrier = pltpu.get_barrier_semaphore()
    peers = (yp, ym, sib) + near["x"] + near["z"]
    for dev in peers:
        pl.semaphore_signal(barrier, inc=1, device_id=dev, device_id_type=MESH)
    pl.semaphore_wait(barrier, len(peers))

    lane = lax.broadcasted_iota(jnp.int32, (8, 128), 1)
    has = jnp.zeros((8, 128), F32)
    for j in range(ids.shape[1]):
        has = has + jnp.where(lane == ids[0, j], 1.0, 0.0)
    pres[0, 0] = has
    p_p = send(pres.at[0, 0], pres.at[3, 0], yp)
    p_m = send(pres.at[0, 0], pres.at[1, 0], ym)
    p_s = send(pres.at[0, 0], pres.at[0, 1], sib)

    own = (tok, cot)
    top_p, bot_p, top_m, bot_m, to_sib = {}, {}, {}, {}, {}
    for a in range(2):
        top_p[a] = send(own[a].at[TOP], A.at[a, 3, 0, TOP], yp)
        bot_m[a] = send(own[a].at[BOTTOM], A.at[a, 1, 0, BOTTOM], ym)
        bot_p[a] = send(own[a].at[BOTTOM], A.at[a, 3, 0, BOTTOM], yp)
        top_m[a] = send(own[a].at[TOP], A.at[a, 1, 0, TOP], ym)
        to_sib[a] = send(own[a], A.at[a, 0, 1], sib)
    loads = [
        local(tok, A.at[0, 0, 0], 0),
        local(cot, A.at[1, 0, 0], 1),
        local(dn, dnv.at[pl.ds(0, slab_rows)], 2),
        local(up, upv.at[pl.ds(0, slab_rows)], 3),
    ]
    for w in (dnv, upv):
        w[pl.ds(slab_rows, ROWS_PAD - slab_rows)] = jnp.zeros((ROWS_PAD - slab_rows, width), BF16)

    arrived(p_p)
    p_f = send(pres.at[3, 0], pres.at[2, 0], yp)
    p_s3 = send(pres.at[3, 0], pres.at[3, 1], sib)
    arrived(p_m)
    p_s1 = send(pres.at[1, 0], pres.at[1, 1], sib)
    arrived(p_f)
    p_s2 = send(pres.at[2, 0], pres.at[2, 1], sib)
    for i in (p_s, p_s3, p_s1, p_s2):
        arrived(i)

    for c in loads:
        c.wait()

    def activations(r):
        def columns(n, carry):
            rows = pl.ds(pl.multiple_of(n * 256, 256), 256)
            nt = (((1,), (1,)), ((), ()))
            s = lax.dot_general(
                A[0, r].reshape(256, width), dnv[rows, :], nt, preferred_element_type=F32
            )
            b = lax.dot_general(
                A[1, r].reshape(256, width), upv[rows, :], nt, preferred_element_type=F32
            )
            block = lax.broadcasted_iota(jnp.int32, (128, 256), 0) - e * 15
            column = lax.broadcasted_iota(jnp.int32, (128, 256), 1) + n * 256
            within = (column >= block * 64) & (column < block * 64 + 64)
            spread = jnp.where(within & (column < slab_rows), 1.0, 0.0).astype(BF16)
            live = [
                jnp.broadcast_to(
                    jnp.dot(pres[r, j].astype(BF16), spread, preferred_element_type=F32)[0:1],
                    (128, 256),
                )
                for j in range(2)
            ]
            live = jnp.concatenate(live, axis=0) > 0.5
            sig = 1.0 / (1.0 + jnp.exp(-s))
            h = s * sig
            g = b * (sig * (1.0 + s * (1.0 - sig)))
            HB[0, pl.ds(r * 256, 256), rows] = jnp.where(live, h, 0.0).astype(BF16)
            HB[1, pl.ds(r * 256, 256), rows] = jnp.where(live, g, 0.0).astype(BF16)
            return carry

        lax.fori_loop(0, ROWS_PAD // 256, columns, 0)

        def turn(d, carry):
            cols = pl.ds(pl.multiple_of(d * 256, 256), 256)
            for a in range(2):
                T[a, cols, pl.ds(r * 256, 256)] = A[a, r, :, :, cols].reshape(256, 256).T
            return carry

        lax.fori_loop(0, width // 256, turn, 0)

    def partials(r):
        def columns(d, carry):
            cols = pl.ds(pl.multiple_of(d * 256, 256), 256)
            for a, w in ((0, upv), (1, dnv)):
                v = jnp.dot(HB[a, pl.ds(r * 256, 256), :], w[:, cols], preferred_element_type=F32)
                A[a, r, :, :, cols] = v.astype(BF16).reshape(2, 128, 256)
            return carry

        lax.fori_loop(0, width // 256, columns, 0)

    def gradient(i):
        _, table, groups = CHUNKS[i]
        G = grads[i][0]

        def rows(q, carry):
            d = pl.ds(pl.multiple_of(q * zs * 64, zs * 64), zs * 64)
            c = pl.ds(groups[0] * 128, len(groups) * 128)

            def term(a):
                return jnp.dot(T[a, d, :], HB[1 - a, :, c], preferred_element_type=F32)

            if table < 2:
                v = term(table)
            else:
                low = lax.broadcasted_iota(jnp.int32, (zs * 64, 128), 1) < 64
                v = jnp.where(low, term(0), pltpu.roll(term(1), 64, 1))
            for j in range(len(groups)):
                G[j, q] = v[:, j * 128 : (j + 1) * 128].astype(BF16).reshape(zs, 64, 128)
            return carry

        lax.fori_loop(0, xs, rows, 0)

    def ring(axis, part, R):
        me, n = spot[axis]
        m = n // 2
        plus, minus = near[axis]
        h0, h1 = pl.ds(0, 32), pl.ds(32, 32)

        def rows_of(ref, h):
            return ref.at[(slice(None),) * (len(ref.shape) - 2) + (h,)]

        far = part((me + m) % n)
        hop_p = send(rows_of(far, h0), rows_of(R.at[0, 0], h0), plus)
        hop_m = send(rows_of(far, h1), rows_of(R.at[1, 0], h1), minus)
        for s in range(1, m):
            yield
            arrived(hop_p)
            to = part((me + m - s) % n)
            src = R.at[0, s - 1]
            if s == 1:
                rows_of(to, h0)[...] += rows_of(src, h0)[...]
            else:
                to[...] += src[...]
            hop_p = send(to, R.at[0, s], plus)
            arrived(hop_m)
            to = part((me + n - m + s) % n)
            src = R.at[1, s - 1]
            if s == 1:
                rows_of(to, h1)[...] += rows_of(src, h1)[...]
            else:
                to[...] += src[...]
            hop_m = send(to, R.at[1, s], minus)
        yield
        arrived(hop_p)
        arrived(hop_m)

    def reduce(i):
        first, table, groups = CHUNKS[i]
        G, Ra, Rb = grads[i]
        if first == "x":
            second = "z"

            def part(d):
                return G.at[:, d]

            def subpart(d):
                return G.at[:, x, d]
        else:
            second = "x"

            def part(d):
                return G.at[:, :, d]

            def subpart(d):
                return G.at[:, d, z]

        me, n = spot[first]
        yield from ring(first, part, Ra)
        mine = part(me)
        m = n // 2
        if m > 1:
            mine[...] = (
                mine[...].astype(F32) + Ra[0, m - 1].astype(F32) + Ra[1, m - 1].astype(F32)
            ).astype(BF16)
        else:
            for side in range(2):
                h = pl.ds(32 * side, 32)
                mine.at[:, :, h][...] += Ra[side, 0, :, :, h]
        yield from ring(second, subpart, Rb)
        me, n = spot[second]
        m = n // 2
        for j, g in enumerate(groups):
            v = subpart(me)[j].astype(F32)
            if m > 1:
                v = v + Rb[0, m - 1, j].astype(F32) + Rb[1, m - 1, j].astype(F32)
            else:
                v = v + jnp.concatenate([Rb[0, 0, j, 0:32], Rb[1, 0, j, 32:64]], axis=0).astype(F32)
            v = v.T
            if table == 2:
                dg_o[14] = v[0:64]
                ug_o[14] = v[64:128]
            else:
                o = (dg_o, ug_o)[table]
                o[2 * g] = v[0:64]
                o[2 * g + 1] = v[64:128]

    for a in range(2):
        arrived(to_sib[a])
    activations(0)
    partials(0)

    to_s = {}

    def parts_to_sibling(r):
        for a in range(2):
            to_s[a, r] = send(A.at[a, r, 1], sibR.at[a, r], sib)

    parts_to_sibling(0)

    far_top, far_bot, on = {}, {}, {}
    for a in range(2):
        arrived(top_p[a])
        far_top[a] = send(A.at[a, 3, 0, TOP], A.at[a, 2, 0, TOP], yp)
        on[a, 3, 0] = send(A.at[a, 3, 0, TOP], A.at[a, 3, 1, TOP], sib)
        arrived(bot_m[a])
        far_bot[a] = send(A.at[a, 1, 0, BOTTOM], A.at[a, 2, 0, BOTTOM], ym)
        on[a, 1, 1] = send(A.at[a, 1, 0, BOTTOM], A.at[a, 1, 1, BOTTOM], sib)
        arrived(bot_p[a])
        on[a, 3, 1] = send(A.at[a, 3, 0, BOTTOM], A.at[a, 3, 1, BOTTOM], sib)
        arrived(top_m[a])
        on[a, 1, 0] = send(A.at[a, 1, 0, TOP], A.at[a, 1, 1, TOP], sib)

    for r in (3, 1):
        for a in range(2):
            for h in range(2):
                arrived(on[a, r, h])
        activations(r)

    for a in range(2):
        arrived(far_top[a])
        on[a, 2, 0] = send(A.at[a, 2, 0, TOP], A.at[a, 2, 1, TOP], sib)
        arrived(far_bot[a])
        on[a, 2, 1] = send(A.at[a, 2, 0, BOTTOM], A.at[a, 2, 1, BOTTOM], sib)

    def free(r):
        for a in range(2):
            for h in range(2):
                sent(on[a, r, h])
            if r == 3:
                sent(far_top[a])
            if r == 1:
                sent(far_bot[a])

    def chip_sum(a, r):
        arrived(to_s[a, r])
        A[a, r, 0] += sibR[a, r]

    free(3)
    partials(3)
    parts_to_sibling(3)
    free(1)
    partials(1)
    parts_to_sibling(1)

    for a in range(2):
        for h in range(2):
            arrived(on[a, 2, h])
    activations(2)

    last_p, last_m = {}, {}
    for a in range(2):
        chip_sum(a, 3)
        last_m[a, 1] = send(A.at[a, 3, 0, BOTTOM], R2.at[0, a, BOTTOM], ym)
        chip_sum(a, 1)
        last_p[a, 0] = send(A.at[a, 1, 0, TOP], R2.at[1, a, TOP], yp)

    running = []

    def launch(i):
        gradient(i)
        running.append(reduce(i))
        next(running[-1])

    def advance():
        for it in list(running):
            try:
                next(it)
            except StopIteration:
                running.remove(it)

    launch(0)
    launch(1)
    free(2)
    partials(2)
    parts_to_sibling(2)
    launch(2)
    hop_m, hop_p = {}, {}
    for a in range(2):
        chip_sum(a, 2)
        hop_m[a] = send(A.at[a, 2, 0, TOP], R1.at[0, a], ym)
        hop_p[a] = send(A.at[a, 2, 0, BOTTOM], R1.at[1, a], yp)
    for i in range(3, len(CHUNKS)):
        launch(i)
    advance()
    for a in range(2):
        arrived(hop_m[a])
        A[a, 3, 0, TOP] += R1[0, a]
        last_m[a, 0] = send(A.at[a, 3, 0, TOP], R2.at[0, a, TOP], ym)
        arrived(hop_p[a])
        A[a, 1, 0, BOTTOM] += R1[1, a]
        last_p[a, 1] = send(A.at[a, 1, 0, BOTTOM], R2.at[1, a, BOTTOM], yp)
    while running:
        advance()
    for a, o in ((0, out_o), (1, in_o)):
        arrived(to_s[a, 0])
        for h in range(2):
            arrived(last_m[a, h])
            arrived(last_p[a, h])
        total = A[a, 0, 0].astype(F32) + sibR[a, 0].astype(F32)
        total = total + R2[0, a].astype(F32) + R2[1, a].astype(F32)
        o[...] = total.astype(BF16)
    for i in range(len(started)):
        sent(i)


def body(xs, zs, tokens, cotangent, down, up, ids):
    blocks, size, width = down.shape
    tile = tokens.shape[0]
    half = len(CHUNKS)
    vmem = pl.BlockSpec(memory_space=pltpu.VMEM)
    scratch = [
        pltpu.VMEM((ROWS_PAD, width), BF16),
        pltpu.VMEM((ROWS_PAD, width), BF16),
        pltpu.VMEM((2, 4, 2, tile, width), BF16),
        pltpu.VMEM((2, width, 8 * tile), BF16),
        pltpu.VMEM((2, 8 * tile, ROWS_PAD), BF16),
        pltpu.VMEM((4, 2, 8, 128), F32),
        pltpu.VMEM((2, 4, tile, width), BF16),
        pltpu.VMEM((2, 2, tile // 2, width), BF16),
        pltpu.VMEM((2, 2, tile, width), BF16),
    ]
    for first, _, groups in CHUNKS:
        g = len(groups)
        scratch.append(pltpu.VMEM((g, xs, zs, 64, 128), BF16))
        if first == "x":
            scratch.append(pltpu.VMEM((2, xs // 2, g, zs, 64, 128), BF16))
            scratch.append(pltpu.VMEM((2, zs // 2, g, 64, 128), BF16))
        else:
            scratch.append(pltpu.VMEM((2, zs // 2, g, xs, 64, 128), BF16))
            scratch.append(pltpu.VMEM((2, xs // 2, g, 64, 128), BF16))
    scratch += [
        pltpu.SemaphoreType.DMA((200,)),
        pltpu.SemaphoreType.DMA((200,)),
        pltpu.SemaphoreType.DMA((4,)),
    ]
    any_spec = pl.BlockSpec(memory_space=pl.ANY)
    return tuple(
        pl.pallas_call(
            functools.partial(kernel, xs, zs),
            out_shape=(
                jax.ShapeDtypeStruct((tile, width), BF16),
                jax.ShapeDtypeStruct((tile, width), BF16),
                jax.ShapeDtypeStruct((blocks, size, width // (xs * zs)), F32),
                jax.ShapeDtypeStruct((blocks, size, width // (xs * zs)), F32),
            ),
            in_specs=[pl.BlockSpec(memory_space=pltpu.SMEM)] + [any_spec] * 4,
            out_specs=(vmem,) * 4,
            scratch_shapes=scratch,
            compiler_params=pltpu.CompilerParams(
                collective_id=0, has_side_effects=True, vmem_limit_bytes=62 * 1024 * 1024
            ),
        )(
            ids,
            tokens,
            cotangent,
            down.reshape(blocks * size, width),
            up.reshape(blocks * size, width),
        )
    )


def solution(mesh):
    placed = (
        P(("dp", "expert"), None),
        P(("dp", "expert"), None),
        P("expert", None, None),
        P("expert", None, None),
        P(("dp", "expert"), None),
    )
    zs = min(ZSIZE, mesh.shape["dp"])
    return jax.shard_map(
        functools.partial(body, mesh.shape["dp"] // zs, zs),
        mesh=mesh,
        in_specs=placed,
        out_specs=(
            P(("dp", "expert"), None),
            P(("dp", "expert"), None),
            P("expert", None, "dp"),
            P("expert", None, "dp"),
        ),
        check_vma=False,
    )
```

```python
import functools

import jax
import jax.numpy as jnp
from jax import lax
from jax.experimental import pallas as pl
from jax.experimental.pallas import tpu as pltpu
from jax.sharding import PartitionSpec as P

MESH = pl.DeviceIdType.MESH
BF16 = jnp.bfloat16
F32 = jnp.float32
ROWS_PAD = 1024
ZSIZE = 8
SLICE = 480
TOP, BOTTOM = pl.ds(0, 64), pl.ds(64, 64)
DOWN = (("x", 0, 2), ("x", 2, 4), ("x", 4, 6), ("x", 6, 8))
RATE, RATE_SIB, DELAY, DELAY_SIB = 44.5, 350.0, 2.0, 1.0


def rows_in(lo, hi):
    return pl.ds(lo * 64, min(hi * 64, SLICE) - lo * 64)


def kernel(xs, zs, *refs):
    ids, tok, cot, dn, up, out_o, in_o, dg_o, ug_o = refs[:9]
    dnv, upv, A, O, T, HB, pres, sibR, R1, R2, G, Rz, Rx = refs[9:22]
    rest = refs[22:]
    down_recv = [rest[2 * i : 2 * i + 2] for i in range(len(DOWN))]
    ssem, rsem, lsem = rest[2 * len(DOWN) :]
    width = tok.shape[1]
    slab_rows = dn.shape[0]
    quarter = width // xs
    row_step = quarter

    dp, e = lax.axis_index("dp"), lax.axis_index("expert")
    x, z = dp // zs, dp % zs
    y, k = e // 2, e % 2
    target = {
        "yp": (dp, ((y + 1) % 4) * 2 + k),
        "ym": (dp, ((y + 3) % 4) * 2 + k),
        "sib": (dp, y * 2 + (1 - k)),
        "xp": (((x + 1) % xs) * zs + z, e),
        "xm": (((x + xs - 1) % xs) * zs + z, e),
        "zp": (x * zs + (z + 1) % zs, e),
        "zm": (x * zs + (z + zs - 1) % zs, e),
    }
    spot = {"x": (x, xs), "z": (z, zs)}

    clock = [0.0]
    link_free = dict.fromkeys(target, 0.0)
    copies, landed, left, got, gone, events = [], [], [], set(), set(), {}
    steps = []

    def send(src, dst, to):
        i = len(copies)
        c = pltpu.make_async_remote_copy(
            src_ref=src, dst_ref=dst, send_sem=ssem.at[i], recv_sem=rsem.at[i],
            device_id=target[to], device_id_type=MESH,
        )
        c.start()
        kb = 1.0
        for d in src.shape:
            kb *= d
        kb *= jnp.dtype(src.dtype).itemsize / 1000
        begin = max(clock[0], link_free[to])
        link_free[to] = begin + kb / (RATE_SIB if to == "sib" else RATE)
        copies.append(c)
        left.append(link_free[to])
        landed.append(link_free[to] + (DELAY_SIB if to == "sib" else DELAY))
        return i

    def spend(us):
        clock[0] += us

    def mark(*name):
        events[name] = clock[0]

    def when(token):
        if isinstance(token, int):
            return landed[token]
        if token[0] == "sent":
            return left[token[1]]
        return events.get(token, float("inf"))

    def wait(token):
        if isinstance(token, int):
            if token not in got:
                got.add(token)
                copies[token].wait_recv()
        elif token[0] == "sent" and token[1] not in gone:
            gone.add(token[1])
            copies[token[1]].wait_send()

    def add(rank, step):
        steps.append([rank, step, next(step)])

    def run():
        while steps:
            ready = [max([when(t) for t in s[2]], default=0.0) for s in steps]
            now = [i for i in range(len(steps)) if ready[i] <= clock[0]]
            if now:
                i = min(now, key=lambda i: (steps[i][0], ready[i]))
            else:
                i = min(range(len(steps)), key=lambda i: ready[i])
                clock[0] = ready[i]
            assert ready[i] < float("inf")
            for t in steps[i][2]:
                wait(t)
            try:
                steps[i][2] = next(steps[i][1])
            except StopIteration:
                del steps[i]

    loads = []
    for i, (src, dst) in enumerate(
        (
            (tok, A.at[0, 0, 0]),
            (dn, dnv.at[pl.ds(0, slab_rows)]),
            (cot, A.at[1, 0, 0]),
            (up, upv.at[pl.ds(0, slab_rows)]),
        )
    ):
        loads.append(pltpu.make_async_copy(src, dst, lsem.at[i]))
        loads[-1].start()
    barrier = pltpu.get_barrier_semaphore()
    for dev in target.values():
        pl.semaphore_signal(barrier, inc=1, device_id=dev, device_id_type=MESH)

    lane = lax.broadcasted_iota(jnp.int32, (8, 128), 1)
    has = jnp.zeros((8, 128), F32)
    for j in range(ids.shape[1]):
        has = has + jnp.where(lane == ids[0, j], 1.0, 0.0)
    pres[0, 0] = has
    pl.semaphore_wait(barrier, len(target))

    half = {3: TOP, 1: BOTTOM}
    other = {3: BOTTOM, 1: TOP}
    ahead = {3: "yp", 1: "ym"}
    pres_sib = send(pres.at[0, 0], pres.at[0, 1], "sib")
    pres_near = {r: send(pres.at[0, 0], pres.at[r, 0], ahead[r]) for r in (3, 1)}
    near = {}
    for r in (3, 1):
        near[r, 0] = send(tok.at[half[r]], A.at[0, r, 0, half[r]], ahead[r])
    tok_sib = send(tok, A.at[0, 0, 1], "sib")
    for r in (3, 1):
        near[r, 1] = send(tok.at[other[r]], A.at[0, r, 0, other[r]], ahead[r])
    cot_sib = send(cot, A.at[1, 0, 1], "sib")
    for w in (dnv, upv):
        w[pl.ds(slab_rows, ROWS_PAD - slab_rows)] = jnp.zeros((ROWS_PAD - slab_rows, width), BF16)

    far, cots, on = {}, {}, {}

    def quarter_of(q):
        return pl.ds(q * quarter, quarter)

    def send_cot(r, q):
        for h in (half[r], other[r]):
            cots[r, q, h is other[r]] = send(
                cot.at[h, quarter_of(q)], A.at[1, r, 0, h, quarter_of(q)], ahead[r]
            )
        mark("cot out", r, q)

    def pass_presence(r):
        yield [pres_near[r]]
        if r == 3:
            far["pres"] = send(pres.at[3, 0], pres.at[2, 0], "yp")
            mark("far pres")
        on["pres", r] = send(pres.at[r, 0], pres.at[r, 1], "sib")
        mark("pres", r)

    def pass_far_presence():
        yield [("far pres",)]
        yield [far["pres"]]
        on["pres", 2] = send(pres.at[2, 0], pres.at[2, 1], "sib")
        mark("pres", 2)

    def pass_tokens(r):
        yield [near[r, 0]]
        far[r] = send(A.at[0, r, 0, half[r]], A.at[0, 2, 0, half[r]], ahead[r])
        mark("far", r)
        on[0, r, 0] = send(A.at[0, r, 0, half[r]], A.at[0, r, 1, half[r]], "sib")
        send_cot(r, 0)
        if xs > 1:
            send_cot(r, 1)
        yield [near[r, 1]]
        on[0, r, 1] = send(A.at[0, r, 0, other[r]], A.at[0, r, 1, other[r]], "sib")
        mark("tok", r)

    def pass_far_tokens():
        yield [("far", 3), ("far", 1)]
        for r in (3, 1):
            yield [far[r]]
            on[0, 2, r] = send(A.at[0, 2, 0, half[r]], A.at[0, 2, 1, half[r]], "sib")
        mark("tok", 2)

    def pass_cot(r):
        for q in range(xs):
            yield [("cot out", r, q)]
            yield [cots[r, q, False]]
            far[r, q] = send(
                A.at[1, r, 0, half[r], quarter_of(q)], A.at[1, 2, 0, half[r], quarter_of(q)], ahead[r]
            )
            mark("far cot", r, q)
            if q + 2 < xs:
                send_cot(r, q + 2)
            yield [cots[r, q, True]]
            on[1, r, q] = send(
                A.at[1, r, 0, :, quarter_of(q)], A.at[1, r, 1, :, quarter_of(q)], "sib"
            )
            mark("cot", r, q)

    def pass_far_cot():
        for q in range(xs):
            yield [("far cot", 3, q), ("far cot", 1, q)]
            yield [far[3, q], far[1, q]]
            on[1, 2, q] = send(
                A.at[1, 2, 0, :, quarter_of(q)], A.at[1, 2, 1, :, quarter_of(q)], "sib"
            )
            mark("cot", 2, q)

    def rows_of(r):
        return pl.ds(r * 256, 256)

    nt = (((1,), (1,)), ((), ()))

    def scores(r):
        def columns(n, carry):
            cols = pl.ds(pl.multiple_of(n * 256, 256), 256)
            s = lax.dot_general(
                A[0, r].reshape(256, width), dnv[cols, :], nt, preferred_element_type=F32
            )
            block = lax.broadcasted_iota(jnp.int32, (128, 256), 0) - e * 15
            column = lax.broadcasted_iota(jnp.int32, (128, 256), 1) + n * 256
            within = (column >= block * 64) & (column < block * 64 + 64)
            spread = jnp.where(within & (column < slab_rows), 1.0, 0.0).astype(BF16)
            live = [
                jnp.broadcast_to(
                    jnp.dot(pres[r, j].astype(BF16), spread, preferred_element_type=F32)[0:1],
                    (128, 256),
                )
                for j in range(2)
            ]
            live = jnp.concatenate(live, axis=0) > 0.5
            sig = 1.0 / (1.0 + jnp.exp(-s))
            slope = sig * (1.0 + s * (1.0 - sig))
            HB[0, rows_of(r), cols] = jnp.where(live, s * sig, 0.0).astype(BF16)
            HB[1, rows_of(r), cols] = jnp.where(live, slope, 0.0).astype(BF16)
            return carry

        lax.fori_loop(0, ROWS_PAD // 256, columns, 0)
        spend(1.8)

    def back(r):
        def columns(n, carry):
            cols = pl.ds(pl.multiple_of(n * 256, 256), 256)
            b = lax.dot_general(
                A[1, r].reshape(256, width), upv[cols, :], nt, preferred_element_type=F32
            )
            HB[1, rows_of(r), cols] = (b * HB[1, rows_of(r), cols].astype(F32)).astype(BF16)
            return carry

        lax.fori_loop(0, ROWS_PAD // 256, columns, 0)
        spend(1.6)

    def turn(a, r, lo, hi):
        def columns(d, carry):
            cols = pl.ds(pl.multiple_of(d * 128, 128), 128)
            T[a, cols, rows_of(r)] = A[a, r, :, :, cols].reshape(256, 128).T
            return carry

        lax.fori_loop(lo // 128, hi // 128, columns, 0)
        spend(0.6 * (hi - lo) / width)

    def parts_of(a, r):
        return O.at[a, r // 2] if r in (3, 1) else A.at[a, r]

    def partial(a, r):
        w = (upv, dnv)[a]
        to = parts_of(a, r)

        def columns(d, carry):
            cols = pl.ds(pl.multiple_of(d * 256, 256), 256)
            v = jnp.dot(HB[a, rows_of(r), :], w[:, cols], preferred_element_type=F32)
            to[:, :, cols] = v.astype(BF16).reshape(2, 128, 256)
            return carry

        lax.fori_loop(0, width // 256, columns, 0)
        spend(1.9)

    def gradient(table, q, pair):
        d = pl.ds(pl.multiple_of(q * row_step, row_step), row_step)
        c = pl.ds(pl.multiple_of(pair * 256, 256), 256)
        v = jnp.dot(T[table, d, :], HB[1 - table, :, c], preferred_element_type=F32)
        for j in range(2):
            w = v[:, j * 128 : (j + 1) * 128]
            w = w.reshape(zs, 64, 128)
            if j == 1 and isinstance(pair, int) and pair == 3:
                low = w[:, 32:64].reshape(zs * 32, 128)
                w = w[:, 0:32] + pltpu.roll(low, 64, 1).reshape(zs, 32, 128)
                G[table, q, :, pl.ds(448, 32)] = w.astype(BF16)
            else:
                g = pl.ds(pl.multiple_of(pair * 128 + j * 64, 64), 64)
                G[table, q, :, g] = w.astype(BF16)

    def emit(v, o, lo, hi):
        for g in range(lo, hi):
            w = v[(g - lo) * 64 : (g - lo) * 64 + (64 if g < 7 else 32)]
            if g < 7:
                w = w.T
                o[2 * g] = w[0:64]
                o[2 * g + 1] = w[64:128]
            else:
                w = jnp.concatenate([w, pltpu.roll(w, 64, 1)], axis=0).T
                o[14] = w[0:64]

    def halves(ref, side):
        rows = ref.shape[-2] // 2
        return ref.at[(slice(None),) * (len(ref.shape) - 2) + (pl.ds(side * rows, rows),)]

    def one_way(name, axis, part, R, side):
        me, n = spot[axis]
        m = n // 2
        to = axis + "pm"[side]
        here = part((me + m) % n)
        hop = send(halves(here, side), halves(R.at[side, 0], side), to)
        for s in range(1, m):
            yield [hop]
            here = part((me + m - s) % n if side == 0 else (me + n - m + s) % n)
            src = R.at[side, s - 1]
            if s == 1:
                halves(here, side)[...] += halves(src, side)[...]
            else:
                here[...] += src[...]
            spend(0.2)
            hop = send(here, R.at[side, s], to)
        yield [hop]
        mark("ring", name, side)

    def ring(name, axis, part, R):
        for side in range(2):
            add(0, one_way(name, axis, part, R, side))
        return [("ring", name, side) for side in range(2)]

    def total(axis, part, R):
        me, n = spot[axis]
        m = n // 2
        v = part(me)[...].astype(F32)
        if m > 1:
            return v + R[0, m - 1].astype(F32) + R[1, m - 1].astype(F32)
        rows = v.shape[-2] // 2
        r0, r1 = R[0, 0].astype(F32), R[1, 0].astype(F32)
        return v + jnp.concatenate([r0[..., :rows, :], r1[..., rows:, :]], axis=-2)

    ready_up = []

    def up_quarter(q):
        yield [("scores", r) for r in range(4)] + [cot_sib]
        for r in (0, 3, 1, 2):
            if r:
                yield [("cot", r, q)]
                yield [on[1, r, q]]
            turn(1, r, q * quarter, (q + 1) * quarter)
        mark("turned", q)

        def pairs(n, carry):
            gradient(1, q, n)
            return carry

        lax.fori_loop(0, 3, pairs, 0)
        gradient(1, q, 3)
        spend(1.8)

        def part(d):
            return G.at[1, q, d]

        yield ring(("up", q), "z", part, Rz.at[q])
        G[1, q, z] = total("z", part, Rz.at[q]).astype(BF16)
        spend(0.2)
        mark("up z", q)

    def up_rest():
        yield [("up z", q) for q in range(xs)]

        def part(d):
            return G.at[1, d, z]

        yield ring("up x", "x", part, Rx)
        emit(total("x", part, Rx), ug_o, 0, 8)
        spend(0.5)

    def down_chunk(i):
        first, lo, hi = DOWN[i]
        rows = rows_in(lo, hi)
        yield [("back", r) for r in range(4)]

        def loop(q, carry):
            gradient(0, q, lo // 2)
            return carry

        lax.fori_loop(0, xs, loop, 0)
        spend(1.8)
        Ra, Rb = down_recv[i]
        if first == "x":
            part, second, sub = (lambda d: G.at[0, d, :, rows]), "z", (lambda d: G.at[0, x, d, rows])
        else:
            part, second, sub = (lambda d: G.at[0, :, d, rows]), "x", (lambda d: G.at[0, d, z, rows])
        yield ring(("down", i), first, part, Ra)
        part(spot[first][0])[...] = total(first, part, Ra).astype(BF16)
        spend(0.2)
        yield ring(("down 2", i), second, sub, Rb)
        emit(total(second, sub, Rb), dg_o, lo, hi)
        spend(0.3)

    def forward(r):
        if r == 0:
            yield [tok_sib, pres_sib]
            for c in loads[:2]:
                c.wait()
        else:
            yield [("tok", r), ("pres", r)]
            pair = [on[0, 2, 3], on[0, 2, 1]] if r == 2 else [on[0, r, 0], on[0, r, 1]]
            yield pair + [on["pres", r]] + ([pres_near[r]] if r != 2 else [far["pres"]])
        scores(r)
        mark("scores", r)
        turn(0, r, 0, width)
        mark("turned tok", r)

    def forward_out(r):
        yield [("turned tok", r), ("loaded",)]
        if r == 2:
            yield [("sent", on[0, 2, 3]), ("sent", on[0, 2, 1])]
        partial(0, r)
        send_parts(0, r)

    def load_rest():
        yield []
        for c in loads[2:]:
            c.wait()
        mark("loaded")

    def backward(r):
        yield [("scores", r), ("loaded",)]
        if r == 0:
            yield [cot_sib]
        else:
            yield [("cot", r, q) for q in range(xs)]
            yield [on[1, r, q] for q in range(xs)]
        back(r)
        mark("back", r)

    def backward_out(r):
        yield [("back", r)] + [("turned", q) for q in range(xs)] * (r in (0, 2))
        if r == 2:
            yield [("sent", on[1, 2, q]) for q in range(xs)]
        partial(1, r)
        send_parts(1, r)

    to_sib, hop, last = {}, {}, {}

    def send_parts(a, r):
        to_sib[a, r] = send(parts_of(a, r).at[1], sibR.at[a, r], "sib")
        mark("parts", a, r)

    side_of = {3: 0, 1: 1}
    back_to = {3: "ym", 1: "yp"}

    def chip_sum(a, r):
        yield [("parts", a, r)]
        yield [to_sib[a, r]]
        parts_of(a, r).at[0][...] += sibR[a, r]
        spend(0.2)
        mark("sum", a, r)
        if r == 0:
            return
        yield [("far cot", 3, xs - 1), ("far cot", 1, xs - 1)]
        if r == 2:
            hop[a, 3] = send(A.at[a, 2, 0, TOP], R1.at[0, a], "ym")
            hop[a, 1] = send(A.at[a, 2, 0, BOTTOM], R1.at[1, a], "yp")
            mark("hop", a)
        else:
            h = other[r]
            last[a, r, 0] = send(parts_of(a, r).at[0, h], R2.at[side_of[r], a, h], back_to[r])
            mark("last", a, r, 0)

    def pass_sum(a, r):
        yield [("sum", a, r), ("hop", a), ("last", a, r, 0)]
        yield [hop[a, r]]
        h = half[r]
        parts_of(a, r).at[0, h][...] += R1[side_of[r], a]
        spend(0.1)
        last[a, r, 1] = send(parts_of(a, r).at[0, h], R2.at[side_of[r], a, h], back_to[r])
        mark("last", a, r, 1)

    def finish(a, o):
        yield [("sum", a, 0)] + [("last", a, r, i) for r in (3, 1) for i in range(2)]
        yield [last[a, r, i] for r in (3, 1) for i in range(2)]
        v = A[a, 0, 0].astype(F32) + R2[0, a].astype(F32) + R2[1, a].astype(F32)
        o[...] = v.astype(BF16)
        spend(0.4)

    for r in (3, 1):
        add(0, pass_presence(r))
    add(0, pass_far_presence())
    for r in (3, 1):
        add(0, pass_tokens(r))
    add(0, pass_far_tokens())
    for r in (3, 1):
        add(0, pass_cot(r))
    add(0, pass_far_cot())
    for r in (0, 3, 1, 2):
        add(1, forward(r))
    add(2, load_rest())
    for q in range(xs):
        add(2, up_quarter(q))
    add(6, up_rest())
    for r in (0, 3, 1, 2):
        add(3, backward(r))
    for i in range(len(DOWN)):
        add(3 if i < 2 else 5, down_chunk(i))
    for r in (0, 3, 1, 2):
        add(4, forward_out(r))
        add(4, backward_out(r))
    for a in range(2):
        for r in (2, 3, 1, 0):
            add(1, chip_sum(a, r))
        for r in (3, 1):
            add(0, pass_sum(a, r))
        add(6, finish(a, (out_o, in_o)[a]))
    run()
    for i in range(len(copies)):
        wait(i)
        wait(("sent", i))


def hand_over(*refs):
    sem = refs[12]
    moves = []
    for i in range(4):
        moves.append(pltpu.make_async_copy(refs[i], refs[8 + i], sem.at[i]))
        moves[-1].start()
    for i in range(4):
        moves[i].wait()
        moves.append(pltpu.make_async_copy(refs[8 + i], refs[4 + i], sem.at[4 + i]))
        moves[-1].start()
    for c in moves[4:]:
        c.wait()


def body(xs, zs, tokens, cotangent, down, up, ids):
    blocks, size, width = down.shape
    tile = tokens.shape[0]
    vmem = pl.BlockSpec(memory_space=pltpu.VMEM)
    scratch = [
        pltpu.VMEM((ROWS_PAD, width), BF16),
        pltpu.VMEM((ROWS_PAD, width), BF16),
        pltpu.VMEM((2, 4, 2, tile, width), BF16),
        pltpu.VMEM((2, 2, 2, tile, width), BF16),
        pltpu.VMEM((2, width, 8 * tile), BF16),
        pltpu.VMEM((2, 8 * tile, ROWS_PAD), BF16),
        pltpu.VMEM((4, 2, 8, 128), F32),
        pltpu.VMEM((2, 4, tile, width), BF16),
        pltpu.VMEM((2, 2, tile // 2, width), BF16),
        pltpu.VMEM((2, 2, tile, width), BF16),
        pltpu.VMEM((2, xs, zs, SLICE, 128), BF16),
        pltpu.VMEM((xs, 2, zs // 2, SLICE, 128), BF16),
        pltpu.VMEM((2, xs // 2, SLICE, 128), BF16),
    ]
    for first, lo, hi in DOWN:
        rows = rows_in(lo, hi).size
        if first == "x":
            scratch.append(pltpu.VMEM((2, xs // 2, zs, rows, 128), BF16))
            scratch.append(pltpu.VMEM((2, zs // 2, rows, 128), BF16))
        else:
            scratch.append(pltpu.VMEM((2, zs // 2, xs, rows, 128), BF16))
            scratch.append(pltpu.VMEM((2, xs // 2, rows, 128), BF16))
    scratch += [
        pltpu.SemaphoreType.DMA((256,)),
        pltpu.SemaphoreType.DMA((256,)),
        pltpu.SemaphoreType.DMA((4,)),
    ]
    any_spec = pl.BlockSpec(memory_space=pl.ANY)
    shapes = (
        jax.ShapeDtypeStruct((tile, width), BF16),
        jax.ShapeDtypeStruct((tile, width), BF16),
        jax.ShapeDtypeStruct((blocks, size, width // (xs * zs)), F32),
        jax.ShapeDtypeStruct((blocks, size, width // (xs * zs)), F32),
    )
    results = pl.pallas_call(
        functools.partial(kernel, xs, zs),
        out_shape=shapes,
        in_specs=[pl.BlockSpec(memory_space=pltpu.SMEM)] + [any_spec] * 4,
        out_specs=(vmem,) * 4,
        scratch_shapes=scratch,
        compiler_params=pltpu.CompilerParams(
            collective_id=0, has_side_effects=True, vmem_limit_bytes=62 * 1024 * 1024
        ),
    )(
        ids,
        tokens,
        cotangent,
        down.reshape(blocks * size, width),
        up.reshape(blocks * size, width),
    )
    return tuple(
        pl.pallas_call(
            hand_over,
            out_shape=shapes,
            in_specs=[any_spec] * 4,
            out_specs=(any_spec,) * 4,
            scratch_shapes=[pltpu.VMEM(s.shape, s.dtype) for s in shapes]
            + [pltpu.SemaphoreType.DMA((8,))],
        )(*results)
    )


def solution(mesh):
    placed = (
        P(("dp", "expert"), None),
        P(("dp", "expert"), None),
        P("expert", None, None),
        P("expert", None, None),
        P(("dp", "expert"), None),
    )
    zs = min(ZSIZE, mesh.shape["dp"])
    return jax.shard_map(
        functools.partial(body, mesh.shape["dp"] // zs, zs),
        mesh=mesh,
        in_specs=placed,
        out_specs=(
            P(("dp", "expert"), None),
            P(("dp", "expert"), None),
            P("expert", None, "dp"),
            P("expert", None, "dp"),
        ),
        check_vma=False,
    )
```

```python
import functools

import jax
import jax.numpy as jnp
from jax import lax
from jax.experimental import pallas as pl
from jax.experimental.pallas import tpu as pltpu
from jax.sharding import PartitionSpec as P

MESH = pl.DeviceIdType.MESH
BF16 = jnp.bfloat16
F32 = jnp.float32
ROWS_PAD = 1024
ZSIZE = 8
SLICE = 480
TOP, BOTTOM = pl.ds(0, 64), pl.ds(64, 64)
DOWN = (("x", 0, 2), ("x", 2, 4), ("x", 4, 6), ("x", 6, 7), ("z", 7, 8))
FORWARD, BACKWARD = (1, 1.4, 1, 1.2), (2, 1.3, 2.6, 2)
FORWARD_OUT, BACKWARD_OUT = (2.65, 4, 4, 1.5), (3.3, 5, 5, 3.3)
UP_QUARTER = (1.5, 1.9, 3, 3)
DOWN_CHUNK = (2.3, 3.2, 2.3, 2.3, 2.3)
PIECES = 2
RATE, RATE_SIB, DELAY, DELAY_SIB = 44.5, 350.0, 2.0, 1.0


def rows_in(lo, hi):
    return pl.ds(lo * 64, min(hi * 64, SLICE) - lo * 64)


def kernel(xs, zs, *refs):
    ids, tok, cot, dn, up, out_o, in_o, dg_o, ug_o = refs[:9]
    dnv, upv, A, O, T, HB, pres, sibR, R1, R2, G, Rz, Rx = refs[9:22]
    rest = refs[22:]
    down_recv = [rest[2 * i : 2 * i + 2] for i in range(len(DOWN))]
    ssem, rsem, lsem = rest[2 * len(DOWN) :]
    width = tok.shape[1]
    slab_rows = dn.shape[0]
    quarter = width // xs

    dp, e = lax.axis_index("dp"), lax.axis_index("expert")
    x, z = dp // zs, dp % zs
    y, k = e // 2, e % 2
    target = {
        "yp": (dp, ((y + 1) % 4) * 2 + k),
        "ym": (dp, ((y + 3) % 4) * 2 + k),
        "sib": (dp, y * 2 + (1 - k)),
        "xp": (((x + 1) % xs) * zs + z, e),
        "xm": (((x + xs - 1) % xs) * zs + z, e),
        "zp": (x * zs + (z + 1) % zs, e),
        "zm": (x * zs + (z + zs - 1) % zs, e),
    }
    spot = {"x": (x, xs), "z": (z, zs)}

    clock = [0.0]
    link_free = dict.fromkeys(target, 0.0)
    copies, landed, left, got, gone, events = [], [], [], set(), set(), {}
    steps = []

    def send(src, dst, to):
        i = len(copies)
        c = pltpu.make_async_remote_copy(
            src_ref=src, dst_ref=dst, send_sem=ssem.at[i], recv_sem=rsem.at[i],
            device_id=target[to], device_id_type=MESH,
        )
        c.start()
        kb = 1.0
        for d in src.shape:
            kb *= d
        kb *= jnp.dtype(src.dtype).itemsize / 1000
        begin = max(clock[0], link_free[to])
        link_free[to] = begin + kb / (RATE_SIB if to == "sib" else RATE)
        copies.append(c)
        left.append(link_free[to])
        landed.append(link_free[to] + (DELAY_SIB if to == "sib" else DELAY))
        return i

    def spend(us):
        clock[0] += us

    def mark(*name):
        events[name] = clock[0]

    def when(token):
        if isinstance(token, int):
            return landed[token]
        if token[0] == "sent":
            return left[token[1]]
        return events.get(token, float("inf"))

    def wait(token):
        if isinstance(token, int):
            if token not in got:
                got.add(token)
                copies[token].wait_recv()
        elif token[0] == "sent" and token[1] not in gone:
            gone.add(token[1])
            copies[token[1]].wait_send()

    def add(rank, step):
        steps.append([rank, step, next(step)])

    def run():
        while steps:
            ready = [max([when(t) for t in s[2]], default=0.0) for s in steps]
            now = [i for i in range(len(steps)) if ready[i] <= clock[0]]
            if now:
                i = min(now, key=lambda i: (steps[i][0], ready[i]))
            else:
                i = min(range(len(steps)), key=lambda i: ready[i])
                clock[0] = ready[i]
            assert ready[i] < float("inf")
            for t in steps[i][2]:
                wait(t)
            try:
                steps[i][2] = next(steps[i][1])
            except StopIteration:
                del steps[i]

    loads = []
    for i, (src, dst) in enumerate(
        (
            (tok, A.at[0, 0, 0]),
            (dn, dnv.at[pl.ds(0, slab_rows)]),
            (cot, A.at[1, 0, 0]),
            (up, upv.at[pl.ds(0, slab_rows)]),
        )
    ):
        loads.append(pltpu.make_async_copy(src, dst, lsem.at[i]))
        loads[-1].start()
    barrier = pltpu.get_barrier_semaphore()
    for dev in target.values():
        pl.semaphore_signal(barrier, inc=1, device_id=dev, device_id_type=MESH)

    lane = lax.broadcasted_iota(jnp.int32, (8, 128), 1)
    has = jnp.zeros((8, 128), F32)
    for j in range(ids.shape[1]):
        has = has + jnp.where(lane == ids[0, j], 1.0, 0.0)
    pres[0, 0] = has
    pl.semaphore_wait(barrier, len(target))

    half = {3: TOP, 1: BOTTOM}
    other = {3: BOTTOM, 1: TOP}
    ahead = {3: "yp", 1: "ym"}
    pres_sib = send(pres.at[0, 0], pres.at[0, 1], "sib")
    pres_near = {r: send(pres.at[0, 0], pres.at[r, 0], ahead[r]) for r in (3, 1)}
    near = {}
    for r in (3, 1):
        near[r, 0] = send(tok.at[half[r]], A.at[0, r, 0, half[r]], ahead[r])
    tok_sib = send(tok, A.at[0, 0, 1], "sib")
    for r in (3, 1):
        near[r, 1] = send(tok.at[other[r]], A.at[0, r, 0, other[r]], ahead[r])
    cot_sib = send(cot, A.at[1, 0, 1], "sib")
    for w in (dnv, upv):
        w[pl.ds(slab_rows, ROWS_PAD - slab_rows)] = jnp.zeros((ROWS_PAD - slab_rows, width), BF16)

    far, cots, on = {}, {}, {}

    def quarter_of(q):
        return pl.ds(q * quarter, quarter)

    def send_ahead(r, q):
        if q < xs:
            c = quarter_of(q)
            cots[r, q, False] = send(cot.at[half[r], c], A.at[1, r, 0, half[r], c], ahead[r])

    def send_behind(r, q):
        if q < xs:
            c = quarter_of(q)
            cots[r, q, True] = send(cot.at[other[r], c], A.at[1, r, 0, other[r], c], ahead[r])
            mark("cot out", r, q)

    def pass_presence(r):
        yield [pres_near[r]]
        if r == 3:
            far["pres"] = send(pres.at[3, 0], pres.at[2, 0], "yp")
            mark("far pres")
        on["pres", r] = send(pres.at[r, 0], pres.at[r, 1], "sib")
        mark("pres", r)

    def pass_far_presence():
        yield [("far pres",)]
        yield [far["pres"]]
        on["pres", 2] = send(pres.at[2, 0], pres.at[2, 1], "sib")
        mark("pres", 2)

    def pass_tokens(r):
        yield [near[r, 0]]
        far[r] = send(A.at[0, r, 0, half[r]], A.at[0, 2, 0, half[r]], ahead[r])
        mark("far", r)
        on[0, r, 0] = send(A.at[0, r, 0, half[r]], A.at[0, r, 1, half[r]], "sib")
        send_ahead(r, 0)
        send_behind(r, 0)
        send_ahead(r, 1)
        yield [near[r, 1]]
        on[0, r, 1] = send(A.at[0, r, 0, other[r]], A.at[0, r, 1, other[r]], "sib")
        mark("tok", r)

    def pass_far_tokens():
        yield [("far", 3), ("far", 1)]
        for r in (3, 1):
            yield [far[r]]
            on[0, 2, r] = send(A.at[0, 2, 0, half[r]], A.at[0, 2, 1, half[r]], "sib")
        mark("tok", 2)

    def pass_cot(r):
        for q in range(xs):
            if q == 0:
                yield [("cot out", r, 0)]
            yield [cots[r, q, False]]
            far[r, q] = send(
                A.at[1, r, 0, half[r], quarter_of(q)], A.at[1, 2, 0, half[r], quarter_of(q)], ahead[r]
            )
            mark("far cot", r, q)
            if q == 0:
                send_behind(r, 1)
                send_ahead(r, 2)
            if q == 1:
                send_behind(r, 2)
                send_ahead(r, 3)
                send_behind(r, 3)
            yield [cots[r, q, True]]
            on[1, r, q] = send(
                A.at[1, r, 0, :, quarter_of(q)], A.at[1, r, 1, :, quarter_of(q)], "sib"
            )
            mark("cot", r, q)

    def pass_far_cot():
        for q in range(xs):
            yield [("far cot", 3, q), ("far cot", 1, q)]
            yield [far[3, q], far[1, q]]
            on[1, 2, q] = send(
                A.at[1, 2, 0, :, quarter_of(q)], A.at[1, 2, 1, :, quarter_of(q)], "sib"
            )
            mark("cot", 2, q)

    def rows_of(r):
        return pl.ds(r * 256, 256)

    nt = (((1,), (1,)), ((), ()))

    def scores(r):
        def columns(n, carry):
            cols = pl.ds(pl.multiple_of(n * 512, 512), 512)
            s = lax.dot_general(
                A[0, r].reshape(256, width), dnv[cols, :], nt, preferred_element_type=F32
            )
            block = lax.broadcasted_iota(jnp.int32, (128, 512), 0) - e * 15
            column = lax.broadcasted_iota(jnp.int32, (128, 512), 1) + n * 512
            within = (column >= block * 64) & (column < block * 64 + 64)
            spread = jnp.where(within & (column < slab_rows), 1.0, 0.0).astype(BF16)
            live = [
                jnp.broadcast_to(
                    jnp.dot(pres[r, j].astype(BF16), spread, preferred_element_type=F32)[0:1],
                    (128, 512),
                )
                for j in range(2)
            ]
            live = jnp.concatenate(live, axis=0) > 0.5
            sig = 1.0 / (1.0 + jnp.exp(-s))
            slope = sig * (1.0 + s * (1.0 - sig))
            HB[0, rows_of(r), cols] = jnp.where(live, s * sig, 0.0).astype(BF16)
            HB[1, rows_of(r), cols] = jnp.where(live, slope, 0.0).astype(BF16)
            return carry

        yield from cut(ROWS_PAD // 512, 1.6, columns)

    def back(r):
        def columns(n, carry):
            cols = pl.ds(pl.multiple_of(n * 512, 512), 512)
            b = lax.dot_general(
                A[1, r].reshape(256, width), upv[cols, :], nt, preferred_element_type=F32
            )
            HB[1, rows_of(r), cols] = (b * HB[1, rows_of(r), cols].astype(F32)).astype(BF16)
            return carry

        yield from cut(ROWS_PAD // 512, 1.3, columns)

    def turn(a, r, lo, hi):
        step = min(256, hi - lo)

        def columns(d, carry):
            cols = pl.ds(pl.multiple_of(d * step, step), step)
            T[a, cols, rows_of(r)] = A[a, r, :, :, cols].reshape(256, step).T
            return carry

        lax.fori_loop(lo // step, hi // step, columns, 0)
        spend(0.55 * (hi - lo) / width)

    def parts_of(a, r):
        return O.at[a, r // 2] if r in (3, 1) else A.at[a, r]

    def cut(steps, us, loop):
        for i in range(PIECES):
            if i:
                yield []
            lax.fori_loop(steps * i // PIECES, steps * (i + 1) // PIECES, loop, 0)
            spend(us / PIECES)

    def partial(a, r):
        w = (upv, dnv)[a]
        to = parts_of(a, r)

        step = min(width, 1024)

        def columns(d, carry):
            cols = pl.ds(pl.multiple_of(d * step, step), step)
            v = jnp.dot(HB[a, rows_of(r), :], w[:, cols], preferred_element_type=F32)
            to[:, :, cols] = v.astype(BF16).reshape(2, 128, step)
            return carry

        yield from cut(width // step, 1.3, columns)

    def gradient(table, q, lo, hi):
        v = jnp.dot(
            T[table, pl.ds(q * quarter, quarter), :],
            HB[1 - table, :, pl.ds(lo * 128, (hi - lo) * 128)],
            preferred_element_type=F32,
        )
        for g in range(lo, hi):
            w = v[:, (g - lo) * 128 : (g - lo + 1) * 128].reshape(zs, 64, 128)
            if g == 7:
                low = w[:, 32:64].reshape(zs * 32, 128)
                w = w[:, 0:32] + pltpu.roll(low, 64, 1).reshape(zs, 32, 128)
            G[table, q, :, rows_in(g, g + 1)] = w.astype(BF16)

    def emit(v, o, lo, hi):
        for g in range(lo, hi):
            w = v[(g - lo) * 64 : (g - lo) * 64 + (64 if g < 7 else 32)]
            if g < 7:
                w = w.T
                o[2 * g] = w[0:64]
                o[2 * g + 1] = w[64:128]
            else:
                w = jnp.concatenate([w, pltpu.roll(w, 64, 1)], axis=0).T
                o[14] = w[0:64]

    def halves(ref, side):
        rows = ref.shape[-2] // 2
        return ref.at[(slice(None),) * (len(ref.shape) - 2) + (pl.ds(side * rows, rows),)]

    def one_way(name, axis, part, R, side):
        me, n = spot[axis]
        m = n // 2
        to = axis + "pm"[side]
        here = part((me + m) % n)
        hop = send(halves(here, side), halves(R.at[side, 0], side), to)
        for s in range(1, m):
            yield [hop]
            here = part((me + m - s) % n if side == 0 else (me + n - m + s) % n)
            src = R.at[side, s - 1]
            if s == 1:
                halves(here, side)[...] += halves(src, side)[...]
            else:
                here[...] += src[...]
            spend(0.2)
            hop = send(here, R.at[side, s], to)
        yield [hop]
        mark("ring", name, side)

    def ring(name, axis, part, R):
        for side in range(2):
            add(0, one_way(name, axis, part, R, side))
        return [("ring", name, side) for side in range(2)]

    def total(axis, part, R):
        me, n = spot[axis]
        m = n // 2
        v = part(me)[...].astype(F32)
        if m > 1:
            return v + R[0, m - 1].astype(F32) + R[1, m - 1].astype(F32)
        rows = v.shape[-2] // 2
        r0, r1 = R[0, 0].astype(F32), R[1, 0].astype(F32)
        return v + jnp.concatenate([r0[..., :rows, :], r1[..., rows:, :]], axis=-2)

    ready_up = []

    def up_quarter(q):
        yield [("scores", r) for r in range(4)] + [cot_sib]
        for r in (0, 3, 1, 2):
            if r:
                yield [("cot", r, q)]
                yield [on[1, r, q]]
            turn(1, r, q * quarter, (q + 1) * quarter)
        mark("turned", q)
        if PIECES > 1:
            yield []

        gradient(1, q, 0, 8)
        spend(1.2)

        def part(d):
            return G.at[1, q, d]

        yield ring(("up", q), "z", part, Rz.at[q])
        G[1, q, z] = total("z", part, Rz.at[q]).astype(BF16)
        spend(0.2)
        mark("up z", q)

    def up_rest():
        yield [("up z", q) for q in range(xs)]

        def part(d):
            return G.at[1, d, z]

        yield ring("up x", "x", part, Rx)
        emit(total("x", part, Rx), ug_o, 0, 8)
        spend(0.5)

    def down_chunk(i):
        first, lo, hi = DOWN[i]
        rows = rows_in(lo, hi)
        yield [("back", r) for r in range(4)]

        for q in range(xs):
            gradient(0, q, lo, hi)
        spend(0.6 * (hi - lo))
        Ra, Rb = down_recv[i]
        if first == "x":
            part, second, sub = (lambda d: G.at[0, d, :, rows]), "z", (lambda d: G.at[0, x, d, rows])
        else:
            part, second, sub = (lambda d: G.at[0, :, d, rows]), "x", (lambda d: G.at[0, d, z, rows])
        yield ring(("down", i), first, part, Ra)
        part(spot[first][0])[...] = total(first, part, Ra).astype(BF16)
        spend(0.2)
        yield ring(("down 2", i), second, sub, Rb)
        emit(total(second, sub, Rb), dg_o, lo, hi)
        spend(0.3)

    def forward(r):
        if r == 0:
            yield [tok_sib, pres_sib]
            for c in loads[:2]:
                c.wait()
        else:
            yield [("tok", r), ("pres", r)]
            pair = [on[0, 2, 3], on[0, 2, 1]] if r == 2 else [on[0, r, 0], on[0, r, 1]]
            yield pair + [on["pres", r]] + ([pres_near[r]] if r != 2 else [far["pres"]])
        yield from scores(r)
        mark("scores", r)
        if PIECES > 1:
            yield []
        turn(0, r, 0, width)
        mark("turned tok", r)

    def forward_out(r):
        yield [("turned tok", r), ("loaded",)]
        if r == 2:
            yield [("sent", on[0, 2, 3]), ("sent", on[0, 2, 1])]
        yield from partial(0, r)
        send_parts(0, r)

    def load_rest():
        yield []
        for c in loads[2:]:
            c.wait()
        mark("loaded")

    def backward(r):
        yield [("scores", r), ("loaded",)]
        if r == 0:
            yield [cot_sib]
        else:
            yield [("cot", r, q) for q in range(xs)]
            yield [on[1, r, q] for q in range(xs)]
        yield from back(r)
        mark("back", r)

    def backward_out(r):
        yield [("back", r)] + [("turned", q) for q in range(xs)] * (r in (0, 2))
        if r == 2:
            yield [("sent", on[1, 2, q]) for q in range(xs)]
        yield from partial(1, r)
        send_parts(1, r)

    to_sib, hop, last = {}, {}, {}

    def send_parts(a, r):
        to_sib[a, r] = send(parts_of(a, r).at[1], sibR.at[a, r], "sib")
        mark("parts", a, r)

    side_of = {3: 0, 1: 1}
    back_to = {3: "ym", 1: "yp"}

    def chip_sum(a, r):
        yield [("parts", a, r)]
        yield [to_sib[a, r]]
        parts_of(a, r).at[0][...] += sibR[a, r]
        spend(0.2)
        mark("sum", a, r)
        if r == 0:
            return
        yield [("far cot", 3, xs - 1), ("far cot", 1, xs - 1)]
        if r == 2:
            hop[a, 3] = send(A.at[a, 2, 0, TOP], R1.at[0, a], "ym")
            hop[a, 1] = send(A.at[a, 2, 0, BOTTOM], R1.at[1, a], "yp")
            mark("hop", a)
        else:
            h = other[r]
            last[a, r, 0] = send(parts_of(a, r).at[0, h], R2.at[side_of[r], a, h], back_to[r])
            mark("last", a, r, 0)

    def pass_sum(a, r):
        yield [("sum", a, r), ("hop", a), ("last", a, r, 0)]
        yield [hop[a, r]]
        h = half[r]
        parts_of(a, r).at[0, h][...] += R1[side_of[r], a]
        spend(0.1)
        last[a, r, 1] = send(parts_of(a, r).at[0, h], R2.at[side_of[r], a, h], back_to[r])
        mark("last", a, r, 1)

    def finish(a, o):
        yield [("sum", a, 0)] + [("last", a, r, i) for r in (3, 1) for i in range(2)]
        yield [last[a, r, i] for r in (3, 1) for i in range(2)]
        v = A[a, 0, 0].astype(F32) + R2[0, a].astype(F32) + R2[1, a].astype(F32)
        o[...] = v.astype(BF16)
        spend(0.4)

    for r in (3, 1):
        add(0, pass_presence(r))
    add(0, pass_far_presence())
    for r in (3, 1):
        add(0, pass_tokens(r))
    add(0, pass_far_tokens())
    for r in (3, 1):
        add(0, pass_cot(r))
    add(0, pass_far_cot())
    add(2, load_rest())
    for i, r in enumerate((0, 3, 1, 2)):
        add(FORWARD[i], forward(r))
        add(BACKWARD[i], backward(r))
        add(FORWARD_OUT[i], forward_out(r))
        add(BACKWARD_OUT[i], backward_out(r))
    for q in range(xs):
        add(UP_QUARTER[q], up_quarter(q))
    add(6, up_rest())
    for i in range(len(DOWN)):
        add(DOWN_CHUNK[i], down_chunk(i))
    for a in range(2):
        for r in (2, 3, 1, 0):
            add(1, chip_sum(a, r))
        for r in (3, 1):
            add(0, pass_sum(a, r))
        add(6, finish(a, (out_o, in_o)[a]))
    run()
    for i in range(len(copies)):
        wait(i)
        wait(("sent", i))


def hand_over(*refs):
    sem = refs[12]
    moves = []
    for i in range(4):
        moves.append(pltpu.make_async_copy(refs[i], refs[8 + i], sem.at[i]))
        moves[-1].start()
    for i in range(4):
        moves[i].wait()
        moves.append(pltpu.make_async_copy(refs[8 + i], refs[4 + i], sem.at[4 + i]))
        moves[-1].start()
    for c in moves[4:]:
        c.wait()


def body(xs, zs, tokens, cotangent, down, up, ids):
    blocks, size, width = down.shape
    tile = tokens.shape[0]
    vmem = pl.BlockSpec(memory_space=pltpu.VMEM)
    scratch = [
        pltpu.VMEM((ROWS_PAD, width), BF16),
        pltpu.VMEM((ROWS_PAD, width), BF16),
        pltpu.VMEM((2, 4, 2, tile, width), BF16),
        pltpu.VMEM((2, 2, 2, tile, width), BF16),
        pltpu.VMEM((2, width, 8 * tile), BF16),
        pltpu.VMEM((2, 8 * tile, ROWS_PAD), BF16),
        pltpu.VMEM((4, 2, 8, 128), F32),
        pltpu.VMEM((2, 4, tile, width), BF16),
        pltpu.VMEM((2, 2, tile // 2, width), BF16),
        pltpu.VMEM((2, 2, tile, width), BF16),
        pltpu.VMEM((2, xs, zs, SLICE, 128), BF16),
        pltpu.VMEM((xs, 2, zs // 2, SLICE, 128), BF16),
        pltpu.VMEM((2, xs // 2, SLICE, 128), BF16),
    ]
    for first, lo, hi in DOWN:
        rows = rows_in(lo, hi).size
        if first == "x":
            scratch.append(pltpu.VMEM((2, xs // 2, zs, rows, 128), BF16))
            scratch.append(pltpu.VMEM((2, zs // 2, rows, 128), BF16))
        else:
            scratch.append(pltpu.VMEM((2, zs // 2, xs, rows, 128), BF16))
            scratch.append(pltpu.VMEM((2, xs // 2, rows, 128), BF16))
    scratch += [
        pltpu.SemaphoreType.DMA((256,)),
        pltpu.SemaphoreType.DMA((256,)),
        pltpu.SemaphoreType.DMA((4,)),
    ]
    any_spec = pl.BlockSpec(memory_space=pl.ANY)
    shapes = (
        jax.ShapeDtypeStruct((tile, width), BF16),
        jax.ShapeDtypeStruct((tile, width), BF16),
        jax.ShapeDtypeStruct((blocks, size, width // (xs * zs)), F32),
        jax.ShapeDtypeStruct((blocks, size, width // (xs * zs)), F32),
    )
    results = pl.pallas_call(
        functools.partial(kernel, xs, zs),
        out_shape=shapes,
        in_specs=[pl.BlockSpec(memory_space=pltpu.SMEM)] + [any_spec] * 4,
        out_specs=(vmem,) * 4,
        scratch_shapes=scratch,
        compiler_params=pltpu.CompilerParams(
            collective_id=0, has_side_effects=True, vmem_limit_bytes=62 * 1024 * 1024
        ),
    )(
        ids,
        tokens,
        cotangent,
        down.reshape(blocks * size, width),
        up.reshape(blocks * size, width),
    )
    return tuple(
        pl.pallas_call(
            hand_over,
            out_shape=shapes,
            in_specs=[any_spec] * 4,
            out_specs=(any_spec,) * 4,
            scratch_shapes=[pltpu.VMEM(s.shape, s.dtype) for s in shapes]
            + [pltpu.SemaphoreType.DMA((8,))],
        )(*results)
    )


def solution(mesh):
    placed = (
        P(("dp", "expert"), None),
        P(("dp", "expert"), None),
        P("expert", None, None),
        P("expert", None, None),
        P(("dp", "expert"), None),
    )
    zs = min(ZSIZE, mesh.shape["dp"])
    return jax.shard_map(
        functools.partial(body, mesh.shape["dp"] // zs, zs),
        mesh=mesh,
        in_specs=placed,
        out_specs=(
            P(("dp", "expert"), None),
            P(("dp", "expert"), None),
            P("expert", None, "dp"),
            P("expert", None, "dp"),
        ),
        check_vma=False,
    )
```

```python
import functools

import jax
import jax.numpy as jnp
from jax import lax
from jax.experimental import pallas as pl
from jax.experimental.pallas import tpu as pltpu
from jax.sharding import PartitionSpec as P

MESH = pl.DeviceIdType.MESH
BF16 = jnp.bfloat16
F32 = jnp.float32
ROWS_PAD = 1024
ZSIZE = 8
SLICE = 480
TOP, BOTTOM = pl.ds(0, 64), pl.ds(64, 64)
DOWN = (("x", 0, 2), ("x", 2, 4), ("x", 4, 6), ("x", 6, 7), ("z", 7, 8))
UP = ((0, 5), (5, 8))
FORWARD, BACKWARD = (1, 1.4, 1, 1.2), (2, 1.3, 1.3, 2)
FORWARD_OUT, BACKWARD_OUT = (2.65, 4, 4, 4), (3.3, 3.3, 5, 3.3)
UP_QUARTER = (2.1, 1.9, 2.5, 3)
DOWN_CHUNK = (2.3, 2.3, 2.3, 2.3, 3.2)
PIECES = 2
RATE, RATE_SIB, DELAY, DELAY_SIB = 44.5, 350.0, 2.0, 1.0


def rows_in(lo, hi):
    return pl.ds(lo * 64, min(hi * 64, SLICE) - lo * 64)


def kernel(xs, zs, *refs):
    ids, tok, cot, dn, up, out_o, in_o, dg_o, ug_o = refs[:9]
    dnv, upv, A, O, T, HB, pres, sibR, R1, R2, G, Rz, Rx = refs[9:22]
    rest = refs[22:]
    down_recv = [rest[2 * i : 2 * i + 2] for i in range(len(DOWN))]
    ssem, rsem, lsem = rest[2 * len(DOWN) :]
    width = tok.shape[1]
    slab_rows = dn.shape[0]
    quarter = width // xs

    dp, e = lax.axis_index("dp"), lax.axis_index("expert")
    x, z = dp // zs, dp % zs
    y, k = e // 2, e % 2
    target = {
        "yp": (dp, ((y + 1) % 4) * 2 + k),
        "ym": (dp, ((y + 3) % 4) * 2 + k),
        "sib": (dp, y * 2 + (1 - k)),
        "xp": (((x + 1) % xs) * zs + z, e),
        "xm": (((x + xs - 1) % xs) * zs + z, e),
        "zp": (x * zs + (z + 1) % zs, e),
        "zm": (x * zs + (z + zs - 1) % zs, e),
    }
    spot = {"x": (x, xs), "z": (z, zs)}

    clock = [0.0]
    link_free = dict.fromkeys(target, 0.0)
    copies, landed, left, got, gone, events = [], [], [], set(), set(), {}
    steps = []

    def send(src, dst, to):
        i = len(copies)
        c = pltpu.make_async_remote_copy(
            src_ref=src, dst_ref=dst, send_sem=ssem.at[i], recv_sem=rsem.at[i],
            device_id=target[to], device_id_type=MESH,
        )
        c.start()
        kb = 1.0
        for d in src.shape:
            kb *= d
        kb *= jnp.dtype(src.dtype).itemsize / 1000
        begin = max(clock[0], link_free[to])
        link_free[to] = begin + kb / (RATE_SIB if to == "sib" else RATE)
        copies.append(c)
        left.append(link_free[to])
        landed.append(link_free[to] + (DELAY_SIB if to == "sib" else DELAY))
        return i

    def spend(us):
        clock[0] += us

    def mark(*name):
        events[name] = clock[0]

    def when(token):
        if isinstance(token, int):
            return landed[token]
        if token[0] == "sent":
            return left[token[1]]
        return events.get(token, float("inf"))

    def wait(token):
        if isinstance(token, int):
            if token not in got:
                got.add(token)
                copies[token].wait_recv()
        elif token[0] == "sent" and token[1] not in gone:
            gone.add(token[1])
            copies[token[1]].wait_send()

    def add(rank, step):
        steps.append([rank, step, next(step)])

    def run():
        while steps:
            ready = [max([when(t) for t in s[2]], default=0.0) for s in steps]
            now = [i for i in range(len(steps)) if ready[i] <= clock[0]]
            if now:
                i = min(now, key=lambda i: (steps[i][0], ready[i]))
            else:
                i = min(range(len(steps)), key=lambda i: ready[i])
                clock[0] = ready[i]
            assert ready[i] < float("inf")
            for t in steps[i][2]:
                wait(t)
            try:
                steps[i][2] = next(steps[i][1])
            except StopIteration:
                del steps[i]

    loads = []
    for i, (src, dst) in enumerate(
        (
            (tok, A.at[0, 0, 0]),
            (dn, dnv.at[pl.ds(0, slab_rows)]),
            (cot, A.at[1, 0, 0]),
            (up, upv.at[pl.ds(0, slab_rows)]),
        )
    ):
        loads.append(pltpu.make_async_copy(src, dst, lsem.at[i]))
        loads[-1].start()
    barrier = pltpu.get_barrier_semaphore()
    for dev in target.values():
        pl.semaphore_signal(barrier, inc=1, device_id=dev, device_id_type=MESH)

    lane = lax.broadcasted_iota(jnp.int32, (8, 128), 1)
    has = jnp.zeros((8, 128), F32)
    for j in range(ids.shape[1]):
        has = has + jnp.where(lane == ids[0, j], 1.0, 0.0)
    pres[0, 0] = has
    pl.semaphore_wait(barrier, len(target))

    half = {3: TOP, 1: BOTTOM}
    other = {3: BOTTOM, 1: TOP}
    ahead = {3: "yp", 1: "ym"}
    pres_sib = send(pres.at[0, 0], pres.at[0, 1], "sib")
    pres_near = {r: send(pres.at[0, 0], pres.at[r, 0], ahead[r]) for r in (3, 1)}
    near = {}
    for r in (3, 1):
        near[r, 0] = send(tok.at[half[r]], A.at[0, r, 0, half[r]], ahead[r])
    tok_sib = send(tok, A.at[0, 0, 1], "sib")
    for r in (3, 1):
        near[r, 1] = send(tok.at[other[r]], A.at[0, r, 0, other[r]], ahead[r])
    cot_sib = send(cot, A.at[1, 0, 1], "sib")
    for w in (dnv, upv):
        w[pl.ds(slab_rows, ROWS_PAD - slab_rows)] = jnp.zeros((ROWS_PAD - slab_rows, width), BF16)

    far, cots, on = {}, {}, {}

    def quarter_of(q):
        return pl.ds(q * quarter, quarter)

    def send_ahead(r, q):
        if q < xs:
            c = quarter_of(q)
            cots[r, q, False] = send(cot.at[half[r], c], A.at[1, r, 0, half[r], c], ahead[r])

    def send_behind(r, q):
        if q < xs:
            c = quarter_of(q)
            cots[r, q, True] = send(cot.at[other[r], c], A.at[1, r, 0, other[r], c], ahead[r])
            mark("cot out", r, q)

    def pass_presence(r):
        yield [pres_near[r]]
        if r == 3:
            far["pres"] = send(pres.at[3, 0], pres.at[2, 0], "yp")
            mark("far pres")
        on["pres", r] = send(pres.at[r, 0], pres.at[r, 1], "sib")
        mark("pres", r)

    def pass_far_presence():
        yield [("far pres",)]
        yield [far["pres"]]
        on["pres", 2] = send(pres.at[2, 0], pres.at[2, 1], "sib")
        mark("pres", 2)

    def pass_tokens(r):
        yield [near[r, 0]]
        far[r] = send(A.at[0, r, 0, half[r]], A.at[0, 2, 0, half[r]], ahead[r])
        mark("far", r)
        on[0, r, 0] = send(A.at[0, r, 0, half[r]], A.at[0, r, 1, half[r]], "sib")
        send_ahead(r, 0)
        send_behind(r, 0)
        send_ahead(r, 1)
        yield [near[r, 1]]
        on[0, r, 1] = send(A.at[0, r, 0, other[r]], A.at[0, r, 1, other[r]], "sib")
        mark("tok", r)

    def pass_far_tokens():
        yield [("far", 3), ("far", 1)]
        for r in (3, 1):
            yield [far[r]]
            on[0, 2, r] = send(A.at[0, 2, 0, half[r]], A.at[0, 2, 1, half[r]], "sib")
        mark("tok", 2)

    def pass_cot(r):
        for q in range(xs):
            if q == 0:
                yield [("cot out", r, 0)]
            yield [cots[r, q, False]]
            far[r, q] = send(
                A.at[1, r, 0, half[r], quarter_of(q)], A.at[1, 2, 0, half[r], quarter_of(q)], ahead[r]
            )
            mark("far cot", r, q)
            if q == 0:
                send_behind(r, 1)
                send_ahead(r, 2)
            if q == 1:
                send_behind(r, 2)
                send_ahead(r, 3)
                send_behind(r, 3)
            yield [cots[r, q, True]]
            on[1, r, q] = send(
                A.at[1, r, 0, :, quarter_of(q)], A.at[1, r, 1, :, quarter_of(q)], "sib"
            )
            mark("cot", r, q)

    def pass_far_cot():
        for q in range(xs):
            yield [("far cot", 3, q), ("far cot", 1, q)]
            yield [far[3, q], far[1, q]]
            on[1, 2, q] = send(
                A.at[1, 2, 0, :, quarter_of(q)], A.at[1, 2, 1, :, quarter_of(q)], "sib"
            )
            mark("cot", 2, q)

    def rows_of(r):
        return pl.ds(r * 256, 256)

    nt = (((1,), (1,)), ((), ()))

    def scores(r):
        def columns(n, carry):
            cols = pl.ds(pl.multiple_of(n * 512, 512), 512)
            s = lax.dot_general(
                A[0, r].reshape(256, width), dnv[cols, :], nt, preferred_element_type=F32
            )
            block = lax.broadcasted_iota(jnp.int32, (128, 512), 0) - e * 15
            column = lax.broadcasted_iota(jnp.int32, (128, 512), 1) + n * 512
            within = (column >= block * 64) & (column < block * 64 + 64)
            spread = jnp.where(within & (column < slab_rows), 1.0, 0.0).astype(BF16)
            live = [
                jnp.broadcast_to(
                    jnp.dot(pres[r, j].astype(BF16), spread, preferred_element_type=F32)[0:1],
                    (128, 512),
                )
                for j in range(2)
            ]
            live = jnp.concatenate(live, axis=0) > 0.5
            sig = 1.0 / (1.0 + jnp.exp(-s))
            slope = sig * (1.0 + s * (1.0 - sig))
            HB[0, rows_of(r), cols] = jnp.where(live, s * sig, 0.0).astype(BF16)
            HB[1, rows_of(r), cols] = jnp.where(live, slope, 0.0).astype(BF16)
            return carry

        yield from cut(ROWS_PAD // 512, 1.6, columns)

    def back(r):
        def columns(n, carry):
            cols = pl.ds(pl.multiple_of(n * 512, 512), 512)
            b = lax.dot_general(
                A[1, r].reshape(256, width), upv[cols, :], nt, preferred_element_type=F32
            )
            HB[1, rows_of(r), cols] = (b * HB[1, rows_of(r), cols].astype(F32)).astype(BF16)
            return carry

        yield from cut(ROWS_PAD // 512, 1.3, columns)

    def turn(a, r, lo, hi):
        step = min(256, hi - lo)

        def columns(d, carry):
            cols = pl.ds(pl.multiple_of(d * step, step), step)
            T[a, cols, rows_of(r)] = A[a, r, :, :, cols].reshape(256, step).T
            return carry

        lax.fori_loop(lo // step, hi // step, columns, 0)
        spend(0.55 * (hi - lo) / width)

    def parts_of(a, r):
        return O.at[a, r // 2] if r in (3, 1) else A.at[a, r]

    def cut(steps, us, loop):
        for i in range(PIECES):
            if i:
                yield []
            lax.fori_loop(steps * i // PIECES, steps * (i + 1) // PIECES, loop, 0)
            spend(us / PIECES)

    def partial(a, r):
        w = (upv, dnv)[a]
        to = parts_of(a, r)

        step = min(width, 1024)

        def columns(d, carry):
            cols = pl.ds(pl.multiple_of(d * step, step), step)
            v = jnp.dot(HB[a, rows_of(r), :], w[:, cols], preferred_element_type=F32)
            to[:, :, cols] = v.astype(BF16).reshape(2, 128, step)
            return carry

        yield from cut(width // step, 1.3, columns)

    def gradient(table, q, lo, hi):
        v = jnp.dot(
            T[table, pl.ds(q * quarter, quarter), :],
            HB[1 - table, :, pl.ds(lo * 128, (hi - lo) * 128)],
            preferred_element_type=F32,
        )
        for g in range(lo, hi):
            w = v[:, (g - lo) * 128 : (g - lo + 1) * 128].reshape(zs, 64, 128)
            if g == 7:
                low = w[:, 32:64].reshape(zs * 32, 128)
                w = w[:, 0:32] + pltpu.roll(low, 64, 1).reshape(zs, 32, 128)
            G[table, q, :, rows_in(g, g + 1)] = w.astype(BF16)

    def emit(v, o, lo, hi):
        for g in range(lo, hi):
            w = v[(g - lo) * 64 : (g - lo) * 64 + (64 if g < 7 else 32)]
            if g < 7:
                w = w.T
                o[2 * g] = w[0:64]
                o[2 * g + 1] = w[64:128]
            else:
                w = jnp.concatenate([w, pltpu.roll(w, 64, 1)], axis=0).T
                o[14] = w[0:64]

    def halves(ref, side):
        rows = ref.shape[-2] // 2
        return ref.at[(slice(None),) * (len(ref.shape) - 2) + (pl.ds(side * rows, rows),)]

    def one_way(name, axis, part, R, side):
        me, n = spot[axis]
        m = n // 2
        to = axis + "pm"[side]
        here = part((me + m) % n)
        hop = send(halves(here, side), halves(R.at[side, 0], side), to)
        for s in range(1, m):
            yield [hop]
            here = part((me + m - s) % n if side == 0 else (me + n - m + s) % n)
            src = R.at[side, s - 1]
            if s == 1:
                halves(here, side)[...] += halves(src, side)[...]
            else:
                here[...] += src[...]
            spend(0.2)
            hop = send(here, R.at[side, s], to)
        yield [hop]
        mark("ring", name, side)

    def ring(name, axis, part, R):
        for side in range(2):
            add(0, one_way(name, axis, part, R, side))
        return [("ring", name, side) for side in range(2)]

    def total(axis, part, R):
        me, n = spot[axis]
        m = n // 2
        v = part(me)[...].astype(F32)
        if m > 1:
            return v + R[0, m - 1].astype(F32) + R[1, m - 1].astype(F32)
        rows = v.shape[-2] // 2
        r0, r1 = R[0, 0].astype(F32), R[1, 0].astype(F32)
        return v + jnp.concatenate([r0[..., :rows, :], r1[..., rows:, :]], axis=-2)

    ready_up = []

    def up_quarter(q):
        yield [("scores", r) for r in range(4)] + [cot_sib]
        for r in (0, 3, 1, 2):
            if r:
                yield [("cot", r, q)]
                yield [on[1, r, q]]
            turn(1, r, q * quarter, (q + 1) * quarter)
        mark("turned", q)
        if PIECES > 1:
            yield []

        gradient(1, q, 0, 8)
        spend(1.2)

        for j in range(len(UP)):
            add(0, up_columns(q, j))

    def up_columns(q, j):
        rows = rows_in(*UP[j])
        part, R = (lambda d: G.at[1, q, d, rows]), Rz.at[q, :, :, rows]
        yield ring(("up", q, j), "z", part, R)
        part(z)[...] = total("z", part, R).astype(BF16)
        spend(0.1)
        mark("up z", q, j)

    def up_rest(j):
        yield [("up z", q, j) for q in range(xs)]
        rows = rows_in(*UP[j])
        part, R = (lambda d: G.at[1, d, z, rows]), Rx.at[:, :, rows]
        yield ring(("up x", j), "x", part, R)
        emit(total("x", part, R), ug_o, *UP[j])
        spend(0.3)

    def down_chunk(i):
        first, lo, hi = DOWN[i]
        rows = rows_in(lo, hi)
        yield [("back", r) for r in range(4)]

        for q in range(xs):
            gradient(0, q, lo, hi)
        spend(0.6 * (hi - lo))
        Ra, Rb = down_recv[i]
        if first == "x":
            part, second, sub = (lambda d: G.at[0, d, :, rows]), "z", (lambda d: G.at[0, x, d, rows])
        else:
            part, second, sub = (lambda d: G.at[0, :, d, rows]), "x", (lambda d: G.at[0, d, z, rows])
        yield ring(("down", i), first, part, Ra)
        part(spot[first][0])[...] = total(first, part, Ra).astype(BF16)
        spend(0.2)
        yield ring(("down 2", i), second, sub, Rb)
        emit(total(second, sub, Rb), dg_o, lo, hi)
        spend(0.3)

    def forward(r):
        if r == 0:
            yield [tok_sib, pres_sib]
            for c in loads[:2]:
                c.wait()
        else:
            yield [("tok", r), ("pres", r)]
            pair = [on[0, 2, 3], on[0, 2, 1]] if r == 2 else [on[0, r, 0], on[0, r, 1]]
            yield pair + [on["pres", r]] + ([pres_near[r]] if r != 2 else [far["pres"]])
        yield from scores(r)
        mark("scores", r)
        if PIECES > 1:
            yield []
        turn(0, r, 0, width)
        mark("turned tok", r)

    def forward_out(r):
        yield [("turned tok", r), ("loaded",)]
        if r == 2:
            yield [("sent", on[0, 2, 3]), ("sent", on[0, 2, 1])]
        yield from partial(0, r)
        send_parts(0, r)

    def load_rest():
        yield []
        for c in loads[2:]:
            c.wait()
        mark("loaded")

    def backward(r):
        yield [("scores", r), ("loaded",)]
        if r == 0:
            yield [cot_sib]
        else:
            yield [("cot", r, q) for q in range(xs)]
            yield [on[1, r, q] for q in range(xs)]
        yield from back(r)
        mark("back", r)

    def backward_out(r):
        yield [("back", r)] + [("turned", q) for q in range(xs)] * (r in (0, 2))
        if r == 2:
            yield [("sent", on[1, 2, q]) for q in range(xs)]
        yield from partial(1, r)
        send_parts(1, r)

    to_sib, hop, last = {}, {}, {}

    def send_parts(a, r):
        to_sib[a, r] = send(parts_of(a, r).at[1], sibR.at[a, r], "sib")
        mark("parts", a, r)

    side_of = {3: 0, 1: 1}
    back_to = {3: "ym", 1: "yp"}

    def chip_sum(a, r):
        yield [("parts", a, r)]
        yield [to_sib[a, r]]
        parts_of(a, r).at[0][...] += sibR[a, r]
        spend(0.2)
        mark("sum", a, r)
        if r == 0:
            return
        yield [("far cot", 3, xs - 1), ("far cot", 1, xs - 1)]
        if r == 2:
            hop[a, 3] = send(A.at[a, 2, 0, TOP], R1.at[0, a], "ym")
            hop[a, 1] = send(A.at[a, 2, 0, BOTTOM], R1.at[1, a], "yp")
            mark("hop", a)
        else:
            h = other[r]
            last[a, r, 0] = send(parts_of(a, r).at[0, h], R2.at[side_of[r], a, h], back_to[r])
            mark("last", a, r, 0)

    def pass_sum(a, r):
        yield [("sum", a, r), ("hop", a), ("last", a, r, 0)]
        yield [hop[a, r]]
        h = half[r]
        parts_of(a, r).at[0, h][...] += R1[side_of[r], a]
        spend(0.1)
        last[a, r, 1] = send(parts_of(a, r).at[0, h], R2.at[side_of[r], a, h], back_to[r])
        mark("last", a, r, 1)

    def finish(a, o):
        yield [("sum", a, 0)] + [("last", a, r, i) for r in (3, 1) for i in range(2)]
        yield [last[a, r, i] for r in (3, 1) for i in range(2)]
        v = A[a, 0, 0].astype(F32) + R2[0, a].astype(F32) + R2[1, a].astype(F32)
        o[...] = v.astype(BF16)
        spend(0.4)

    for r in (3, 1):
        add(0, pass_presence(r))
    add(0, pass_far_presence())
    for r in (3, 1):
        add(0, pass_tokens(r))
    add(0, pass_far_tokens())
    for r in (3, 1):
        add(0, pass_cot(r))
    add(0, pass_far_cot())
    add(2, load_rest())
    for i, r in enumerate((0, 3, 1, 2)):
        add(FORWARD[i], forward(r))
        add(BACKWARD[i], backward(r))
        add(FORWARD_OUT[i], forward_out(r))
        add(BACKWARD_OUT[i], backward_out(r))
    for q in range(xs):
        add(UP_QUARTER[q], up_quarter(q))
    for j in range(len(UP)):
        add(6, up_rest(j))
    for i in range(len(DOWN)):
        add(DOWN_CHUNK[i], down_chunk(i))
    for a in range(2):
        for r in (2, 3, 1, 0):
            add(1, chip_sum(a, r))
        for r in (3, 1):
            add(0, pass_sum(a, r))
        add(6, finish(a, (out_o, in_o)[a]))
    run()
    for i in range(len(copies)):
        wait(i)
        wait(("sent", i))


def hand_over(*refs):
    sem = refs[12]
    moves = []
    for i in range(4):
        moves.append(pltpu.make_async_copy(refs[i], refs[8 + i], sem.at[i]))
        moves[-1].start()
    for i in range(4):
        moves[i].wait()
        moves.append(pltpu.make_async_copy(refs[8 + i], refs[4 + i], sem.at[4 + i]))
        moves[-1].start()
    for c in moves[4:]:
        c.wait()


def body(xs, zs, tokens, cotangent, down, up, ids):
    blocks, size, width = down.shape
    tile = tokens.shape[0]
    vmem = pl.BlockSpec(memory_space=pltpu.VMEM)
    scratch = [
        pltpu.VMEM((ROWS_PAD, width), BF16),
        pltpu.VMEM((ROWS_PAD, width), BF16),
        pltpu.VMEM((2, 4, 2, tile, width), BF16),
        pltpu.VMEM((2, 2, 2, tile, width), BF16),
        pltpu.VMEM((2, width, 8 * tile), BF16),
        pltpu.VMEM((2, 8 * tile, ROWS_PAD), BF16),
        pltpu.VMEM((4, 2, 8, 128), F32),
        pltpu.VMEM((2, 4, tile, width), BF16),
        pltpu.VMEM((2, 2, tile // 2, width), BF16),
        pltpu.VMEM((2, 2, tile, width), BF16),
        pltpu.VMEM((2, xs, zs, SLICE, 128), BF16),
        pltpu.VMEM((xs, 2, zs // 2, SLICE, 128), BF16),
        pltpu.VMEM((2, xs // 2, SLICE, 128), BF16),
    ]
    for first, lo, hi in DOWN:
        rows = rows_in(lo, hi).size
        if first == "x":
            scratch.append(pltpu.VMEM((2, xs // 2, zs, rows, 128), BF16))
            scratch.append(pltpu.VMEM((2, zs // 2, rows, 128), BF16))
        else:
            scratch.append(pltpu.VMEM((2, zs // 2, xs, rows, 128), BF16))
            scratch.append(pltpu.VMEM((2, xs // 2, rows, 128), BF16))
    scratch += [
        pltpu.SemaphoreType.DMA((256,)),
        pltpu.SemaphoreType.DMA((256,)),
        pltpu.SemaphoreType.DMA((4,)),
    ]
    any_spec = pl.BlockSpec(memory_space=pl.ANY)
    shapes = (
        jax.ShapeDtypeStruct((tile, width), BF16),
        jax.ShapeDtypeStruct((tile, width), BF16),
        jax.ShapeDtypeStruct((blocks, size, width // (xs * zs)), F32),
        jax.ShapeDtypeStruct((blocks, size, width // (xs * zs)), F32),
    )
    results = pl.pallas_call(
        functools.partial(kernel, xs, zs),
        out_shape=shapes,
        in_specs=[pl.BlockSpec(memory_space=pltpu.SMEM)] + [any_spec] * 4,
        out_specs=(vmem,) * 4,
        scratch_shapes=scratch,
        compiler_params=pltpu.CompilerParams(
            collective_id=0, has_side_effects=True, vmem_limit_bytes=62 * 1024 * 1024
        ),
    )(
        ids,
        tokens,
        cotangent,
        down.reshape(blocks * size, width),
        up.reshape(blocks * size, width),
    )
    return tuple(
        pl.pallas_call(
            hand_over,
            out_shape=shapes,
            in_specs=[any_spec] * 4,
            out_specs=(any_spec,) * 4,
            scratch_shapes=[pltpu.VMEM(s.shape, s.dtype) for s in shapes]
            + [pltpu.SemaphoreType.DMA((8,))],
        )(*results)
    )


def solution(mesh):
    placed = (
        P(("dp", "expert"), None),
        P(("dp", "expert"), None),
        P("expert", None, None),
        P("expert", None, None),
        P(("dp", "expert"), None),
    )
    zs = min(ZSIZE, mesh.shape["dp"])
    return jax.shard_map(
        functools.partial(body, mesh.shape["dp"] // zs, zs),
        mesh=mesh,
        in_specs=placed,
        out_specs=(
            P(("dp", "expert"), None),
            P(("dp", "expert"), None),
            P("expert", None, "dp"),
            P("expert", None, "dp"),
        ),
        check_vma=False,
    )
```

```python
import functools

import jax
import jax.numpy as jnp
from jax import lax
from jax.experimental import pallas as pl
from jax.experimental.pallas import tpu as pltpu
from jax.sharding import PartitionSpec as P

MESH = pl.DeviceIdType.MESH
BF16 = jnp.bfloat16
F32 = jnp.float32
ROWS_PAD = 1024
ZSIZE = 8
SLICE = 480
TOP, BOTTOM = pl.ds(0, 64), pl.ds(64, 64)
DOWN = (("x", 0, 2), ("x", 2, 4), ("x", 4, 6), ("x", 6, 7), ("z", 7, 8))
FORWARD, BACKWARD = (1, 1.4, 1, 1.2), (2, 1.3, 2.6, 2)
FORWARD_OUT, BACKWARD_OUT = (2.65, 4, 4, 1.5), (3.3, 5, 5, 3.3)
UP_QUARTER = (1.5, 1.9, 3, 3)
DOWN_CHUNK = (2.3, 3.2, 2.3, 2.3, 2.3)
PIECES = 2
RATE, RATE_SIB, DELAY, DELAY_SIB = 44.0, 300.0, 3.0, 1.5


def rows_in(lo, hi):
    return pl.ds(lo * 64, min(hi * 64, SLICE) - lo * 64)


def kernel(xs, zs, *refs):
    ids, tok, cot, dn, up, out_o, in_o, dg_o, ug_o = refs[:9]
    dnv, upv, A, O, T, HB, pres, sibR, R1, R2, G, Rz, Rx = refs[9:22]
    rest = refs[22:]
    down_recv = [rest[2 * i : 2 * i + 2] for i in range(len(DOWN))]
    ssem, rsem, lsem = rest[2 * len(DOWN) :]
    width = tok.shape[1]
    slab_rows = dn.shape[0]
    quarter = width // xs

    dp, e = lax.axis_index("dp"), lax.axis_index("expert")
    x, z = dp // zs, dp % zs
    y, k = e // 2, e % 2
    target = {
        "yp": (dp, ((y + 1) % 4) * 2 + k),
        "ym": (dp, ((y + 3) % 4) * 2 + k),
        "sib": (dp, y * 2 + (1 - k)),
        "xp": (((x + 1) % xs) * zs + z, e),
        "xm": (((x + xs - 1) % xs) * zs + z, e),
        "zp": (x * zs + (z + 1) % zs, e),
        "zm": (x * zs + (z + zs - 1) % zs, e),
    }
    spot = {"x": (x, xs), "z": (z, zs)}

    clock = [0.0]
    link_free = dict.fromkeys(target, 0.0)
    copies, landed, left, got, gone, events = [], [], [], set(), set(), {}
    steps = []

    def send(src, dst, to):
        i = len(copies)
        c = pltpu.make_async_remote_copy(
            src_ref=src, dst_ref=dst, send_sem=ssem.at[i], recv_sem=rsem.at[i],
            device_id=target[to], device_id_type=MESH,
        )
        c.start()
        kb = 1.0
        for d in src.shape:
            kb *= d
        kb *= jnp.dtype(src.dtype).itemsize / 1000
        begin = max(clock[0], link_free[to])
        link_free[to] = begin + kb / (RATE_SIB if to == "sib" else RATE)
        copies.append(c)
        left.append(link_free[to])
        landed.append(link_free[to] + (DELAY_SIB if to == "sib" else DELAY))
        return i

    def spend(us):
        clock[0] += us

    def mark(*name):
        events[name] = clock[0]

    def when(token):
        if isinstance(token, int):
            return landed[token]
        if token[0] == "sent":
            return left[token[1]]
        return events.get(token, float("inf"))

    def wait(token):
        if isinstance(token, int):
            if token not in got:
                got.add(token)
                copies[token].wait_recv()
        elif token[0] == "sent" and token[1] not in gone:
            gone.add(token[1])
            copies[token[1]].wait_send()

    def add(rank, step):
        steps.append([rank, step, next(step)])

    def run():
        while steps:
            ready = [max([when(t) for t in s[2]], default=0.0) for s in steps]
            now = [i for i in range(len(steps)) if ready[i] <= clock[0]]
            if now:
                i = min(now, key=lambda i: (steps[i][0], ready[i]))
            else:
                i = min(range(len(steps)), key=lambda i: ready[i])
                clock[0] = ready[i]
            assert ready[i] < float("inf")
            for t in steps[i][2]:
                wait(t)
            try:
                steps[i][2] = next(steps[i][1])
            except StopIteration:
                del steps[i]

    loads = []
    for i, (src, dst) in enumerate(
        (
            (tok, A.at[0, 0, 0]),
            (dn, dnv.at[pl.ds(0, slab_rows)]),
            (cot, A.at[1, 0, 0]),
            (up, upv.at[pl.ds(0, slab_rows)]),
        )
    ):
        loads.append(pltpu.make_async_copy(src, dst, lsem.at[i]))
        loads[-1].start()
    barrier = pltpu.get_barrier_semaphore()
    for dev in target.values():
        pl.semaphore_signal(barrier, inc=1, device_id=dev, device_id_type=MESH)

    lane = lax.broadcasted_iota(jnp.int32, (8, 128), 1)
    has = jnp.zeros((8, 128), F32)
    for j in range(ids.shape[1]):
        has = has + jnp.where(lane == ids[0, j], 1.0, 0.0)
    pres[0, 0] = has
    pl.semaphore_wait(barrier, len(target))

    half = {3: TOP, 1: BOTTOM}
    other = {3: BOTTOM, 1: TOP}
    ahead = {3: "yp", 1: "ym"}
    pres_sib = send(pres.at[0, 0], pres.at[0, 1], "sib")
    pres_near = {r: send(pres.at[0, 0], pres.at[r, 0], ahead[r]) for r in (3, 1)}
    near = {}
    for r in (3, 1):
        near[r, 0] = send(tok.at[half[r]], A.at[0, r, 0, half[r]], ahead[r])
    tok_sib = send(tok, A.at[0, 0, 1], "sib")
    for r in (3, 1):
        near[r, 1] = send(tok.at[other[r]], A.at[0, r, 0, other[r]], ahead[r])
    cot_sib = send(cot, A.at[1, 0, 1], "sib")
    for w in (dnv, upv):
        w[pl.ds(slab_rows, ROWS_PAD - slab_rows)] = jnp.zeros((ROWS_PAD - slab_rows, width), BF16)

    far, cots, on = {}, {}, {}

    def quarter_of(q):
        return pl.ds(q * quarter, quarter)

    def send_ahead(r, q):
        if q < xs:
            c = quarter_of(q)
            cots[r, q, False] = send(cot.at[half[r], c], A.at[1, r, 0, half[r], c], ahead[r])

    def send_behind(r, q):
        if q < xs:
            c = quarter_of(q)
            cots[r, q, True] = send(cot.at[other[r], c], A.at[1, r, 0, other[r], c], ahead[r])
            mark("cot out", r, q)

    def pass_presence(r):
        yield [pres_near[r]]
        if r == 3:
            far["pres"] = send(pres.at[3, 0], pres.at[2, 0], "yp")
            mark("far pres")
        on["pres", r] = send(pres.at[r, 0], pres.at[r, 1], "sib")
        mark("pres", r)

    def pass_far_presence():
        yield [("far pres",)]
        yield [far["pres"]]
        on["pres", 2] = send(pres.at[2, 0], pres.at[2, 1], "sib")
        mark("pres", 2)

    def pass_tokens(r):
        yield [near[r, 0]]
        far[r] = send(A.at[0, r, 0, half[r]], A.at[0, 2, 0, half[r]], ahead[r])
        mark("far", r)
        on[0, r, 0] = send(A.at[0, r, 0, half[r]], A.at[0, r, 1, half[r]], "sib")
        send_ahead(r, 0)
        send_behind(r, 0)
        send_ahead(r, 1)
        yield [near[r, 1]]
        on[0, r, 1] = send(A.at[0, r, 0, other[r]], A.at[0, r, 1, other[r]], "sib")
        mark("tok", r)

    def pass_far_tokens():
        yield [("far", 3), ("far", 1)]
        for r in (3, 1):
            yield [far[r]]
            on[0, 2, r] = send(A.at[0, 2, 0, half[r]], A.at[0, 2, 1, half[r]], "sib")
        mark("tok", 2)

    def pass_cot(r):
        for q in range(xs):
            if q == 0:
                yield [("cot out", r, 0)]
            yield [cots[r, q, False]]
            far[r, q] = send(
                A.at[1, r, 0, half[r], quarter_of(q)], A.at[1, 2, 0, half[r], quarter_of(q)], ahead[r]
            )
            mark("far cot", r, q)
            if q == 0:
                send_behind(r, 1)
                send_ahead(r, 2)
            if q == 1:
                send_behind(r, 2)
                send_ahead(r, 3)
                send_behind(r, 3)
            yield [cots[r, q, True]]
            on[1, r, q] = send(
                A.at[1, r, 0, :, quarter_of(q)], A.at[1, r, 1, :, quarter_of(q)], "sib"
            )
            mark("cot", r, q)

    def pass_far_cot():
        for q in range(xs):
            yield [("far cot", 3, q), ("far cot", 1, q)]
            yield [far[3, q], far[1, q]]
            on[1, 2, q] = send(
                A.at[1, 2, 0, :, quarter_of(q)], A.at[1, 2, 1, :, quarter_of(q)], "sib"
            )
            mark("cot", 2, q)

    def rows_of(r):
        return pl.ds(r * 256, 256)

    nt = (((1,), (1,)), ((), ()))

    def scores(r):
        def columns(n, carry):
            cols = pl.ds(pl.multiple_of(n * 512, 512), 512)
            s = lax.dot_general(
                A[0, r].reshape(256, width), dnv[cols, :], nt, preferred_element_type=F32
            )
            block = lax.broadcasted_iota(jnp.int32, (128, 512), 0) - e * 15
            column = lax.broadcasted_iota(jnp.int32, (128, 512), 1) + n * 512
            within = (column >= block * 64) & (column < block * 64 + 64)
            spread = jnp.where(within & (column < slab_rows), 1.0, 0.0).astype(BF16)
            live = [
                jnp.broadcast_to(
                    jnp.dot(pres[r, j].astype(BF16), spread, preferred_element_type=F32)[0:1],
                    (128, 512),
                )
                for j in range(2)
            ]
            live = jnp.concatenate(live, axis=0) > 0.5
            sig = 1.0 / (1.0 + jnp.exp(-s))
            slope = sig * (1.0 + s * (1.0 - sig))
            HB[0, rows_of(r), cols] = jnp.where(live, s * sig, 0.0).astype(BF16)
            HB[1, rows_of(r), cols] = jnp.where(live, slope, 0.0).astype(BF16)
            return carry

        yield from cut(ROWS_PAD // 512, 1.6, columns)

    def back(r):
        def columns(n, carry):
            cols = pl.ds(pl.multiple_of(n * 512, 512), 512)
            b = lax.dot_general(
                A[1, r].reshape(256, width), upv[cols, :], nt, preferred_element_type=F32
            )
            HB[1, rows_of(r), cols] = (b * HB[1, rows_of(r), cols].astype(F32)).astype(BF16)
            return carry

        yield from cut(ROWS_PAD // 512, 1.3, columns)

    def turn(a, r, lo, hi):
        step = min(256, hi - lo)

        def columns(d, carry):
            cols = pl.ds(pl.multiple_of(d * step, step), step)
            T[a, cols, rows_of(r)] = A[a, r, :, :, cols].reshape(256, step).T
            return carry

        lax.fori_loop(lo // step, hi // step, columns, 0)
        spend(0.55 * (hi - lo) / width)

    def parts_of(a, r):
        return O.at[a, r // 2] if r in (3, 1) else A.at[a, r]

    def cut(steps, us, loop):
        for i in range(PIECES):
            if i:
                yield []
            lax.fori_loop(steps * i // PIECES, steps * (i + 1) // PIECES, loop, 0)
            spend(us / PIECES)

    def partial(a, r):
        w = (upv, dnv)[a]
        to = parts_of(a, r)

        step = min(width, 1024)

        def columns(d, carry):
            cols = pl.ds(pl.multiple_of(d * step, step), step)
            v = jnp.dot(HB[a, rows_of(r), :], w[:, cols], preferred_element_type=F32)
            to[:, :, cols] = v.astype(BF16).reshape(2, 128, step)
            return carry

        yield from cut(width // step, 1.3, columns)

    def gradient(table, q, lo, hi):
        v = jnp.dot(
            T[table, pl.ds(q * quarter, quarter), :],
            HB[1 - table, :, pl.ds(lo * 128, (hi - lo) * 128)],
            preferred_element_type=F32,
        )
        for g in range(lo, hi):
            w = v[:, (g - lo) * 128 : (g - lo + 1) * 128].reshape(zs, 64, 128)
            if g == 7:
                low = w[:, 32:64].reshape(zs * 32, 128)
                w = w[:, 0:32] + pltpu.roll(low, 64, 1).reshape(zs, 32, 128)
            G[table, q, :, rows_in(g, g + 1)] = w.astype(BF16)

    def emit(v, o, lo, hi):
        for g in range(lo, hi):
            w = v[(g - lo) * 64 : (g - lo) * 64 + (64 if g < 7 else 32)]
            if g < 7:
                w = w.T
                o[2 * g] = w[0:64]
                o[2 * g + 1] = w[64:128]
            else:
                w = jnp.concatenate([w, pltpu.roll(w, 64, 1)], axis=0).T
                o[14] = w[0:64]

    def halves(ref, side):
        rows = ref.shape[-2] // 2
        return ref.at[(slice(None),) * (len(ref.shape) - 2) + (pl.ds(side * rows, rows),)]

    def one_way(name, axis, part, R, side):
        me, n = spot[axis]
        m = n // 2
        to = axis + "pm"[side]
        here = part((me + m) % n)
        hop = send(halves(here, side), halves(R.at[side, 0], side), to)
        for s in range(1, m):
            yield [hop]
            here = part((me + m - s) % n if side == 0 else (me + n - m + s) % n)
            src = R.at[side, s - 1]
            if s == 1:
                halves(here, side)[...] += halves(src, side)[...]
            else:
                here[...] += src[...]
            spend(0.2)
            hop = send(here, R.at[side, s], to)
        yield [hop]
        mark("ring", name, side)

    def ring(name, axis, part, R):
        for side in range(2):
            add(0, one_way(name, axis, part, R, side))
        return [("ring", name, side) for side in range(2)]

    def total(axis, part, R):
        me, n = spot[axis]
        m = n // 2
        v = part(me)[...].astype(F32)
        if m > 1:
            return v + R[0, m - 1].astype(F32) + R[1, m - 1].astype(F32)
        rows = v.shape[-2] // 2
        r0, r1 = R[0, 0].astype(F32), R[1, 0].astype(F32)
        return v + jnp.concatenate([r0[..., :rows, :], r1[..., rows:, :]], axis=-2)

    ready_up = []

    def up_quarter(q):
        yield [("scores", r) for r in range(4)] + [cot_sib]
        for r in (0, 3, 1, 2):
            if r:
                yield [("cot", r, q)]
                yield [on[1, r, q]]
            turn(1, r, q * quarter, (q + 1) * quarter)
        mark("turned", q)
        if PIECES > 1:
            yield []

        gradient(1, q, 0, 8)
        spend(1.2)

        def part(d):
            return G.at[1, q, d]

        yield ring(("up", q), "z", part, Rz.at[q])
        G[1, q, z] = total("z", part, Rz.at[q]).astype(BF16)
        spend(0.2)
        mark("up z", q)

    def up_rest():
        yield [("up z", q) for q in range(xs)]

        def part(d):
            return G.at[1, d, z]

        yield ring("up x", "x", part, Rx)
        emit(total("x", part, Rx), ug_o, 0, 8)
        spend(0.5)

    def down_chunk(i):
        first, lo, hi = DOWN[i]
        rows = rows_in(lo, hi)
        yield [("back", r) for r in range(4)]

        for q in range(xs):
            gradient(0, q, lo, hi)
        spend(0.6 * (hi - lo))
        Ra, Rb = down_recv[i]
        if first == "x":
            part, second, sub = (lambda d: G.at[0, d, :, rows]), "z", (lambda d: G.at[0, x, d, rows])
        else:
            part, second, sub = (lambda d: G.at[0, :, d, rows]), "x", (lambda d: G.at[0, d, z, rows])
        yield ring(("down", i), first, part, Ra)
        part(spot[first][0])[...] = total(first, part, Ra).astype(BF16)
        spend(0.2)
        yield ring(("down 2", i), second, sub, Rb)
        emit(total(second, sub, Rb), dg_o, lo, hi)
        spend(0.3)

    def forward(r):
        if r == 0:
            yield [tok_sib, pres_sib]
            for c in loads[:2]:
                c.wait()
        else:
            yield [("tok", r), ("pres", r)]
            pair = [on[0, 2, 3], on[0, 2, 1]] if r == 2 else [on[0, r, 0], on[0, r, 1]]
            yield pair + [on["pres", r]] + ([pres_near[r]] if r != 2 else [far["pres"]])
        yield from scores(r)
        mark("scores", r)
        if PIECES > 1:
            yield []
        turn(0, r, 0, width)
        mark("turned tok", r)

    def forward_out(r):
        yield [("turned tok", r), ("loaded",)]
        if r == 2:
            yield [("sent", on[0, 2, 3]), ("sent", on[0, 2, 1])]
        yield from partial(0, r)
        send_parts(0, r)

    def load_rest():
        yield []
        for c in loads[2:]:
            c.wait()
        mark("loaded")

    def backward(r):
        yield [("scores", r), ("loaded",)]
        if r == 0:
            yield [cot_sib]
        else:
            yield [("cot", r, q) for q in range(xs)]
            yield [on[1, r, q] for q in range(xs)]
        yield from back(r)
        mark("back", r)

    def backward_out(r):
        yield [("back", r)] + [("turned", q) for q in range(xs)] * (r in (0, 2))
        if r == 2:
            yield [("sent", on[1, 2, q]) for q in range(xs)]
        yield from partial(1, r)
        send_parts(1, r)

    to_sib, hop, last = {}, {}, {}

    def send_parts(a, r):
        to_sib[a, r] = send(parts_of(a, r).at[1], sibR.at[a, r], "sib")
        mark("parts", a, r)

    side_of = {3: 0, 1: 1}
    back_to = {3: "ym", 1: "yp"}

    def chip_sum(a, r):
        yield [("parts", a, r)]
        yield [to_sib[a, r]]
        parts_of(a, r).at[0][...] += sibR[a, r]
        spend(0.2)
        mark("sum", a, r)
        if r == 0:
            return
        yield [("far cot", 3, xs - 1), ("far cot", 1, xs - 1)]
        if r == 2:
            hop[a, 3] = send(A.at[a, 2, 0, TOP], R1.at[0, a], "ym")
            hop[a, 1] = send(A.at[a, 2, 0, BOTTOM], R1.at[1, a], "yp")
            mark("hop", a)
        else:
            h = other[r]
            last[a, r, 0] = send(parts_of(a, r).at[0, h], R2.at[side_of[r], a, h], back_to[r])
            mark("last", a, r, 0)

    def pass_sum(a, r):
        yield [("sum", a, r), ("hop", a), ("last", a, r, 0)]
        yield [hop[a, r]]
        h = half[r]
        parts_of(a, r).at[0, h][...] += R1[side_of[r], a]
        spend(0.1)
        last[a, r, 1] = send(parts_of(a, r).at[0, h], R2.at[side_of[r], a, h], back_to[r])
        mark("last", a, r, 1)

    def finish(a, o):
        yield [("sum", a, 0)] + [("last", a, r, i) for r in (3, 1) for i in range(2)]
        yield [last[a, r, i] for r in (3, 1) for i in range(2)]
        v = A[a, 0, 0].astype(F32) + R2[0, a].astype(F32) + R2[1, a].astype(F32)
        o[...] = v.astype(BF16)
        spend(0.4)

    for r in (3, 1):
        add(0, pass_presence(r))
    add(0, pass_far_presence())
    for r in (3, 1):
        add(0, pass_tokens(r))
    add(0, pass_far_tokens())
    for r in (3, 1):
        add(0, pass_cot(r))
    add(0, pass_far_cot())
    add(2, load_rest())
    for i, r in enumerate((0, 3, 1, 2)):
        add(FORWARD[i], forward(r))
        add(BACKWARD[i], backward(r))
        add(FORWARD_OUT[i], forward_out(r))
        add(BACKWARD_OUT[i], backward_out(r))
    for q in range(xs):
        add(UP_QUARTER[q], up_quarter(q))
    add(6, up_rest())
    for i in range(len(DOWN)):
        add(DOWN_CHUNK[i], down_chunk(i))
    for a in range(2):
        for r in (2, 3, 1, 0):
            add(1, chip_sum(a, r))
        for r in (3, 1):
            add(0, pass_sum(a, r))
        add(6, finish(a, (out_o, in_o)[a]))
    run()
    for i in range(len(copies)):
        wait(i)
        wait(("sent", i))


def hand_over(*refs):
    sem = refs[12]
    moves = []
    for i in range(4):
        moves.append(pltpu.make_async_copy(refs[i], refs[8 + i], sem.at[i]))
        moves[-1].start()
    for i in range(4):
        moves[i].wait()
        moves.append(pltpu.make_async_copy(refs[8 + i], refs[4 + i], sem.at[4 + i]))
        moves[-1].start()
    for c in moves[4:]:
        c.wait()


def body(xs, zs, tokens, cotangent, down, up, ids):
    blocks, size, width = down.shape
    tile = tokens.shape[0]
    vmem = pl.BlockSpec(memory_space=pltpu.VMEM)
    scratch = [
        pltpu.VMEM((ROWS_PAD, width), BF16),
        pltpu.VMEM((ROWS_PAD, width), BF16),
        pltpu.VMEM((2, 4, 2, tile, width), BF16),
        pltpu.VMEM((2, 2, 2, tile, width), BF16),
        pltpu.VMEM((2, width, 8 * tile), BF16),
        pltpu.VMEM((2, 8 * tile, ROWS_PAD), BF16),
        pltpu.VMEM((4, 2, 8, 128), F32),
        pltpu.VMEM((2, 4, tile, width), BF16),
        pltpu.VMEM((2, 2, tile // 2, width), BF16),
        pltpu.VMEM((2, 2, tile, width), BF16),
        pltpu.VMEM((2, xs, zs, SLICE, 128), BF16),
        pltpu.VMEM((xs, 2, zs // 2, SLICE, 128), BF16),
        pltpu.VMEM((2, xs // 2, SLICE, 128), BF16),
    ]
    for first, lo, hi in DOWN:
        rows = rows_in(lo, hi).size
        if first == "x":
            scratch.append(pltpu.VMEM((2, xs // 2, zs, rows, 128), BF16))
            scratch.append(pltpu.VMEM((2, zs // 2, rows, 128), BF16))
        else:
            scratch.append(pltpu.VMEM((2, zs // 2, xs, rows, 128), BF16))
            scratch.append(pltpu.VMEM((2, xs // 2, rows, 128), BF16))
    scratch += [
        pltpu.SemaphoreType.DMA((256,)),
        pltpu.SemaphoreType.DMA((256,)),
        pltpu.SemaphoreType.DMA((4,)),
    ]
    any_spec = pl.BlockSpec(memory_space=pl.ANY)
    shapes = (
        jax.ShapeDtypeStruct((tile, width), BF16),
        jax.ShapeDtypeStruct((tile, width), BF16),
        jax.ShapeDtypeStruct((blocks, size, width // (xs * zs)), F32),
        jax.ShapeDtypeStruct((blocks, size, width // (xs * zs)), F32),
    )
    results = pl.pallas_call(
        functools.partial(kernel, xs, zs),
        out_shape=shapes,
        in_specs=[pl.BlockSpec(memory_space=pltpu.SMEM)] + [any_spec] * 4,
        out_specs=(vmem,) * 4,
        scratch_shapes=scratch,
        compiler_params=pltpu.CompilerParams(
            collective_id=0, has_side_effects=True, vmem_limit_bytes=62 * 1024 * 1024
        ),
    )(
        ids,
        tokens,
        cotangent,
        down.reshape(blocks * size, width),
        up.reshape(blocks * size, width),
    )
    return tuple(
        pl.pallas_call(
            hand_over,
            out_shape=shapes,
            in_specs=[any_spec] * 4,
            out_specs=(any_spec,) * 4,
            scratch_shapes=[pltpu.VMEM(s.shape, s.dtype) for s in shapes]
            + [pltpu.SemaphoreType.DMA((8,))],
        )(*results)
    )


def solution(mesh):
    placed = (
        P(("dp", "expert"), None),
        P(("dp", "expert"), None),
        P("expert", None, None),
        P("expert", None, None),
        P(("dp", "expert"), None),
    )
    zs = min(ZSIZE, mesh.shape["dp"])
    return jax.shard_map(
        functools.partial(body, mesh.shape["dp"] // zs, zs),
        mesh=mesh,
        in_specs=placed,
        out_specs=(
            P(("dp", "expert"), None),
            P(("dp", "expert"), None),
            P("expert", None, "dp"),
            P("expert", None, "dp"),
        ),
        check_vma=False,
    )
```
